512 devices in a mesh: replica: 64 (over x, z), head: 8 (over y, core).
Axes of the slice: x: 4, y: 4, z: 16, core: 2. Of those that a mesh axis runs over, the one named last changes fastest.
Arguments:
- states: float32 [256, 32, 128, 128], P('replica', 'head'), may hold values from -18 to 18
- partner: int32 [64], replicated, may hold values from 0 to 63, as said below
- send_ids: int32 [64, 2], replicated, may hold values from 0 to 3, as said below
- send_count: int32 [64], replicated, may hold values from 1 to 2, as said below
- prefill_slot: int32 [64], P('replica'), may hold values from 0 to 3
- prompt_len: int32 [64], P('replica'), may hold values from 128 to 512, as said below
- decode_slots: int32 [64, 4], P('replica'), may hold values from 0 to 3, each once within a row
- q_prefill: bfloat16 [32768, 4096], P('replica', 'head'), may hold values from -6 to 6
- k_prefill: bfloat16 [32768, 4096], P('replica', 'head'), may hold values from -6 to 6
- v_prefill: bfloat16 [32768, 4096], P('replica', 'head'), may hold values from -6 to 6
- q_decode: bfloat16 [2, 256, 4096], P(None, 'replica', 'head'), may hold values from -6 to 6
- k_decode: bfloat16 [2, 256, 4096], P(None, 'replica', 'head'), may hold values from -6 to 6
- v_decode: bfloat16 [2, 256, 4096], P(None, 'replica', 'head'), may hold values from -6 to 6
- slopes: float32 [32], P('head'), may hold values from 0.003 to 0.06
- w_out: bfloat16 [4096, 3072], P('head'), may hold values from -0.125 to 0.125
Outputs:
- prefill_out: bfloat16 [32768, 3072], P('replica', 'head')
- decode_out: bfloat16 [2, 256, 3072], P(None, 'replica', 'head')
The draws below stay inside these ranges and needn't reach their ends.
Inputs may be any that keep to these rules, and one draw needn't show every extreme that they name: partner[i] = i XOR m for one number m with 1 <= m < 64, the same for every replica, so replicas form pairs. `send_ids`: each row names 2 different slots. `send_count`: some replica sends 2 requests in every draw. `prompt_len`: some replica has 512 valid tokens in every draw.
All inputs are finite; a program needn't handle non-finite values.
Results may differ from the reference program's by a relative error of at most 0.017.
Values may be sent and summed in bfloat16 or wider, within the bound.
No kernel may reach another device: no remote copies, remote signals or barrier semaphores. Data moves between devices by JAX's collectives and lax.ppermute only.
A program may use at most 64 MiB of HBM per device.

```python
import math
import jax
import jax.numpy as jnp
from jax import lax

HEAD_DEV = 4
DK = 128
DOUT = 3072
BLK = 128
MIG = 2
SLOTS = 4
PRE = 512
HEADS = 32
REQS = 256
TOKENS = 32768
N_REPLICA = 64


def draw_partner(key, part):
    key = jax.random.fold_in(key, 11)
    pattern = jax.random.randint(key, (), 1, N_REPLICA, dtype=jnp.int32)
    return jnp.bitwise_xor(jnp.arange(N_REPLICA, dtype=jnp.int32), pattern)


def draw_send_ids(key, part):
    key = jax.random.fold_in(key, 12)
    scores = jax.random.randint(key, (N_REPLICA, SLOTS), 0, 1 << 20, dtype=jnp.int32) * SLOTS
    scores = scores + jnp.arange(SLOTS, dtype=jnp.int32)[None, :]
    ordering = jnp.argsort(scores, axis=1, stable=True).astype(jnp.int32)
    return ordering[:, :MIG]


def draw_send_count(key, part):
    key = jax.random.fold_in(key, 13)
    first_key, second_key = jax.random.split(key)
    counts = jax.random.randint(first_key, (N_REPLICA,), 1, MIG + 1, dtype=jnp.int32)
    fullest = jax.random.randint(second_key, (), 0, N_REPLICA, dtype=jnp.int32)
    return jnp.where(jnp.arange(N_REPLICA, dtype=jnp.int32) == fullest, MIG, counts).astype(jnp.int32)


def draw_prompt_len(key, part):
    key = jax.random.fold_in(key, 14)
    first_key, second_key = jax.random.split(key)
    lengths = jax.random.randint(first_key, (N_REPLICA,), PRE // 4, PRE + 1, dtype=jnp.int32)
    longest = jax.random.randint(second_key, (), 0, N_REPLICA, dtype=jnp.int32)
    return jnp.where(jnp.arange(N_REPLICA, dtype=jnp.int32) == longest, PRE, lengths).astype(jnp.int32)


def with_ends(array, key, least, largest):
    longest = array.shape.index(max(array.shape))
    spots = []
    for shift in (0, 1):
        where = [jax.random.randint(jax.random.fold_in(key, axis), (), 0, length) for axis, length in enumerate(array.shape)]
        where[longest] = (where[longest] + shift) % array.shape[longest]
        spots.append(tuple(where))
    return array.at[spots[0]].set(least).at[spots[1]].set(largest)


def spiked(array, key, source, target, parts, factor):
    owner, partner = [(jnp.arange(array.shape[axis_at]) // (array.shape[axis_at] // parts)).reshape([-1 if axis == axis_at else 1 for axis in range(array.ndim)]) for axis_at in (source, target)]
    chosen = jax.random.permutation(key, parts)[partner]
    strong = (owner == chosen) | (owner == (partner + parts // 2) % parts)
    return jnp.where(strong, factor * array, array)


def level_of(rng, extent, cuts, smallest, largest):
    factor_of, own = 1.0, jax.random.fold_in(rng, 6)
    for position, blocks in cuts:
        draws = jnp.exp(jax.random.uniform(jax.random.fold_in(own, position), (blocks,), jnp.float32, smallest / len(cuts), largest / len(cuts)))
        factor_of = factor_of * jnp.repeat(draws, extent[position] // blocks).reshape([-1 if axis == position else 1 for axis in range(len(extent))])
    return factor_of


def noise(key, shape, spread, limit, pieces=(), kind=jnp.bfloat16):
    loudness = level_of(key, shape, pieces, -0.22, 0.18) if pieces else 1.0
    entries = jax.random.normal(key, shape, jnp.float32) * spread * loudness
    return jnp.minimum(jnp.maximum(entries, -limit), limit).astype(kind)


def heavy_noise(key, dims, spread, bound, cuts, heavy, kind=jnp.bfloat16):
    values = spread * jax.random.normal(key, dims, jnp.float32)
    if cuts:
        values = values * level_of(key, dims, cuts, -0.22, 0.18)
    return jnp.clip(spiked(values, jax.random.fold_in(key, 3), *heavy), -bound, bound).astype(kind)


def setup_inputs(seed: int = 0) -> dict:
    key_of = jax.random.split(jax.random.key(seed), 16)
    states = noise(key_of[0], (REQS, HEADS, DK, DK), 3.0, 18.0, ((0, 64), (1, 8)), jnp.float32)
    partner = draw_partner(jax.random.fold_in(key_of[15], 71), 0)
    send_ids = draw_send_ids(jax.random.fold_in(key_of[15], 71), 0)
    send_count = draw_send_count(jax.random.fold_in(key_of[15], 71), 0)
    prefill_slot = with_ends(jax.random.randint(key_of[4], (N_REPLICA,), 0, SLOTS), jax.random.fold_in(key_of[4], 1), 0, SLOTS - 1).astype(jnp.int32)
    prompt_len = draw_prompt_len(jax.random.fold_in(key_of[15], 71), 0)
    decode_slots = jax.vmap(lambda own: jax.random.permutation(own, SLOTS))(jax.random.split(key_of[6], N_REPLICA)).reshape((N_REPLICA, SLOTS)).astype(jnp.int32)
    q_prefill = noise(key_of[7], (TOKENS, HEADS * DK), 1.0, 6.0, ((0, 64), (1, 8)))
    k_prefill = noise(key_of[8], (TOKENS, HEADS * DK), 1.0, 6.0, ((0, 64), (1, 8)))
    v_prefill = noise(key_of[9], (TOKENS, HEADS * DK), 1.0, 6.0, ((0, 64), (1, 8)))
    q_decode = noise(key_of[10], (2, REQS, HEADS * DK), 1.0, 6.0, ((1, 64), (2, 8)))
    k_decode = noise(key_of[11], (2, REQS, HEADS * DK), 1.0, 6.0, ((1, 64), (2, 8)))
    v_decode = noise(key_of[12], (2, REQS, HEADS * DK), 1.0, 6.0, ((1, 64), (2, 8)))
    slopes = jnp.clip(jnp.exp(math.log(0.06) - 2.9957322 * jax.random.uniform(key_of[13], (HEADS,), jnp.float32) ** level_of(key_of[13], (HEADS,), ((0, 8),), -0.2, 0.2)), 0.003, 0.06)
    w_out = heavy_noise(key_of[14], (HEADS * DK, DOUT), (HEADS * DK) ** -0.5, 0.125, ((0, 8),), (0, 1, 8, 2.0))
    return {"states": states, "partner": partner, "send_ids": send_ids, "send_count": send_count, "prefill_slot": prefill_slot, "prompt_len": prompt_len, "decode_slots": decode_slots, "q_prefill": q_prefill, "k_prefill": k_prefill, "v_prefill": v_prefill, "q_decode": q_decode, "k_decode": k_decode, "v_decode": v_decode, "slopes": slopes, "w_out": w_out}


EPS = 1e-06

def head_norm(inputs):
    factor = lax.rsqrt(lax.optimization_barrier(jnp.mean(inputs * inputs, axis=-1, keepdims=True)) + EPS)
    return inputs * factor

def prefill_block(memory, inputs, slopes):
    q_block, k_block, v_block, valid_count = inputs
    row_ids = jnp.arange(q_block.shape[0], dtype=jnp.int32)
    places = row_ids.astype(jnp.float32)
    is_valid = row_ids < valid_count
    filled = valid_count.astype(jnp.float32)
    distance = jnp.maximum(places[:, None] - places[None, :], 0.0)
    causal = (row_ids[:, None] >= row_ids[None, :]) & is_valid[None, :]
    damping = jnp.where(causal[None], jnp.exp(-slopes[:, None, None] * distance[None]), 0.0)
    q_float = q_block.astype(jnp.float32)
    k_float = k_block.astype(jnp.float32)
    v_float = v_block.astype(jnp.float32)
    scores = jnp.einsum('rhd,chd->hrc', q_float, k_float)
    attn_weights = lax.optimization_barrier((scores * damping).astype(jnp.bfloat16))
    intra_part = jnp.einsum('hrc,chd->rhd', attn_weights.astype(jnp.float32), v_float)
    leading = jnp.exp(-slopes[None, :] * (places[:, None] + 1.0))
    carried = jnp.einsum('rhd,hde->rhe', q_float, memory, precision=lax.Precision.HIGHEST)
    attended = intra_part + leading[:, :, None] * carried
    trailing = jnp.where(is_valid[:, None], jnp.exp(-slopes[None, :] * jnp.maximum(filled - 1.0 - places, 0.0)[:, None]), 0.0)
    keys_weighted = lax.optimization_barrier((k_float * trailing[:, :, None]).astype(jnp.bfloat16))
    update = jnp.einsum('chd,che->hde', keys_weighted.astype(jnp.float32), v_float)
    memory = jnp.exp(-slopes * filled)[:, None, None] * memory + update
    return (memory, attended)

def project(normed, weights):
    row_count = normed.shape[0]
    groups = normed.reshape(row_count, HEADS // HEAD_DEV, HEAD_DEV * DK).astype(jnp.float32)
    partials = jnp.einsum('rgk,gkn->grn', groups, weights)
    partials = lax.optimization_barrier(partials.astype(jnp.bfloat16))
    return lax.optimization_barrier(jnp.sum(partials.astype(jnp.float32), axis=0)).astype(jnp.bfloat16)

def reference(states, partner, send_ids, send_count, prefill_slot, prompt_len, decode_slots, q_prefill, k_prefill, v_prefill, q_decode, k_decode, v_decode, slopes, w_out):
    grouped = states.reshape(N_REPLICA, SLOTS, HEADS, DK, DK)
    q_pre = q_prefill.reshape(N_REPLICA, PRE, HEADS, DK)
    k_pre = k_prefill.reshape(N_REPLICA, PRE, HEADS, DK)
    v_pre = v_prefill.reshape(N_REPLICA, PRE, HEADS, DK)
    q_dec = q_decode.reshape(2, N_REPLICA, SLOTS, HEADS, DK)
    k_dec = k_decode.reshape(2, N_REPLICA, SLOTS, HEADS, DK)
    v_dec = v_decode.reshape(2, N_REPLICA, SLOTS, HEADS, DK)
    weights = w_out.reshape(HEADS // HEAD_DEV, HEAD_DEV * DK, DOUT).astype(jnp.float32)
    slot_ids = jnp.arange(SLOTS, dtype=jnp.int32)
    blocks = PRE // BLK

    def serve(index):
        mate = partner[index]
        own_states = lax.dynamic_index_in_dim(grouped, index, 0, keepdims=False)
        far_states = lax.dynamic_index_in_dim(grouped, mate, 0, keepdims=False)
        leaving = jnp.zeros((SLOTS,), dtype=jnp.bool_)
        for entry in range(MIG):
            leaving = leaving | (slot_ids == send_ids[index, entry]) & (entry < send_count[index])
        moved = jnp.where(leaving[:, None, None, None], jnp.float32(0.0), own_states)
        for entry in range(MIG):
            landing = (slot_ids == send_ids[mate, entry]) & (entry < send_count[mate])
            moved = jnp.where(landing[:, None, None, None], far_states, moved)
        length = prompt_len[index]
        start_state = lax.dynamic_index_in_dim(moved, prefill_slot[index], 0, keepdims=False)
        counts = jnp.clip(length - jnp.arange(blocks, dtype=jnp.int32) * BLK, 0, BLK).astype(jnp.int32)

        def shaped(source):
            return source[index].reshape(blocks, BLK, HEADS, DK)

        def step_block(memory, inputs):
            return prefill_block(memory, inputs, slopes)
        final_state, attended = lax.scan(step_block, start_state, (shaped(q_pre), shaped(k_pre), shaped(v_pre), counts))
        attended = attended.reshape(PRE, HEADS, DK)
        token_ids = jnp.arange(PRE, dtype=jnp.int32)
        prefill_normed = jnp.where((token_ids < length)[:, None, None], head_norm(attended), 0.0)
        prefill_normed = prefill_normed.astype(jnp.bfloat16).reshape(PRE, HEADS * DK)
        served = lax.dynamic_update_index_in_dim(moved, final_state, prefill_slot[index], 0)
        memory = jnp.take(served, decode_slots[index], axis=0)
        keep_rate = jnp.exp(-slopes)[None, :, None, None]
        decode_parts = []
        for step_index in range(2):
            keys = k_dec[step_index, index].astype(jnp.float32)
            values_now = v_dec[step_index, index].astype(jnp.float32)
            query = q_dec[step_index, index].astype(jnp.float32)
            memory = keep_rate * memory + jnp.einsum('rhd,rhe->rhde', keys, values_now)
            output = jnp.einsum('rhd,rhde->rhe', query, memory, precision=lax.Precision.HIGHEST)
            normed = head_norm(output).astype(jnp.bfloat16).reshape(SLOTS, HEADS * DK)
            decode_parts.append(project(normed, weights))
        return (project(prefill_normed, weights), jnp.stack(decode_parts))
    prefill_all, decode_all = lax.map(serve, jnp.arange(N_REPLICA, dtype=jnp.int32))
    return (prefill_all.reshape(TOKENS, DOUT), jnp.transpose(decode_all, (1, 0, 2, 3)).reshape(2, REQS, DOUT))
```

```python
from functools import partial

import jax
import jax.numpy as jnp
from jax import lax
from jax.experimental import pallas as pl
from jax.experimental.pallas import tpu as pltpu
from jax.sharding import PartitionSpec as P

DK = 128
BLK = 128
EPS = 1e-06
PAD = 16
VMEM_LIMIT = 48 * 1024 * 1024
ORDER = (2, 1, 3, 0)


def params(axes=1):
    return pltpu.CompilerParams(
        dimension_semantics=("arbitrary",) * axes, vmem_limit_bytes=VMEM_LIMIT
    )


def dot(left, right, left_dim=1, right_dim=0):
    return lax.dot_general(
        left, right, (((left_dim,), (right_dim,)), ((), ())), preferred_element_type=jnp.float32
    )


def split_dot(left, right):
    high = right.astype(jnp.bfloat16)
    low = (right - high.astype(jnp.float32)).astype(jnp.bfloat16)
    return dot(left, high) + dot(left, low)


def pack_kernel(own_ref, ids_ref, states_ref, out_ref):
    out_ref[...] = states_ref[...].astype(jnp.bfloat16)


def pack(own, send_ids, states):
    _, heads, rows, cols = states.shape
    count = send_ids.shape[1]
    block = (1, heads, rows, cols)
    return pl.pallas_call(
        pack_kernel,
        out_shape=jax.ShapeDtypeStruct((count, heads, rows, cols), jnp.bfloat16),
        grid_spec=pltpu.PrefetchScalarGridSpec(
            num_scalar_prefetch=2,
            grid=(count,),
            in_specs=[pl.BlockSpec(block, lambda j, own, ids: (ids[own[0], j], 0, 0, 0))],
            out_specs=pl.BlockSpec(block, lambda j, own, ids: (j, 0, 0, 0)),
        ),
        compiler_params=params(),
        name="pack",
    )(own, send_ids, states)


def intra_kernel(len_ref, slopes_ref, q_ref, k_ref, v_ref, att_ref, mem_ref):
    slope = slopes_ref[pl.program_id(0)]
    length = len_ref[0]
    rows = lax.broadcasted_iota(jnp.int32, (BLK, BLK), 0)
    cols = lax.broadcasted_iota(jnp.int32, (BLK, BLK), 1)
    damping = jnp.exp(-slope * jnp.maximum(rows - cols, 0).astype(jnp.float32))
    leading = jnp.exp(-slope * (rows + 1).astype(jnp.float32))
    mem_ref[...] = jnp.zeros_like(mem_ref)

    def step(block, carry):
        count = jnp.clip(length - block * BLK, 0, BLK)
        here = pl.ds(pl.multiple_of(block * BLK, BLK), BLK)
        q_block, k_block, v_block = q_ref[here, :], k_ref[here, :], v_ref[here, :]
        memory = mem_ref[0]
        scores = dot(q_block, k_block, 1, 1)
        kept = (cols <= rows) & (cols < count)
        probs = jnp.where(kept, scores * damping, 0.0).astype(jnp.bfloat16)
        att_ref[here, :] = dot(probs, v_block) + leading * split_dot(q_block, memory)
        behind = jnp.maximum(count - 1 - rows, 0).astype(jnp.float32)
        trailing = jnp.where(rows < count, jnp.exp(-slope * behind), 0.0)
        weighted = (k_block.astype(jnp.float32) * trailing).astype(jnp.bfloat16)
        fade = jnp.exp(jnp.full((1, DK), -slope * count.astype(jnp.float32)))
        mem_ref[0] = fade * memory + dot(weighted, v_block, 0, 0)
        return carry

    lax.fori_loop(0, q_ref.shape[0] // BLK, step, 0)


def intra(prompt_len, slopes, q_prefill, k_prefill, v_prefill):
    tokens, width = q_prefill.shape
    heads = width // DK
    column = pl.BlockSpec((tokens, DK), lambda h: (0, h))
    scalar = pl.BlockSpec(memory_space=pltpu.SMEM)
    return pl.pallas_call(
        intra_kernel,
        out_shape=(
            jax.ShapeDtypeStruct((tokens, width), jnp.float32),
            jax.ShapeDtypeStruct((heads, DK, DK), jnp.float32),
        ),
        grid=(heads,),
        in_specs=[scalar, scalar, column, column, column],
        out_specs=(column, pl.BlockSpec((1, DK, DK), lambda h: (h, 0, 0))),
        compiler_params=params(),
        cost_estimate=pl.CostEstimate(
            flops=10 * tokens * BLK * width, bytes_accessed=5 * tokens * width * 2, transcendentals=0
        ),
        name="intra",
    )(prompt_len, slopes, q_prefill, k_prefill, v_prefill)


def head_norm(inputs):
    return inputs * lax.rsqrt(jnp.mean(inputs * inputs, axis=-1, keepdims=True) + EPS)


def serve_kernel(
    place_ref, partner_ref, ids_ref, count_ref, slot_ref, len_ref, decode_ref, slopes_ref,
    states_ref, payload_ref, att_ref, mem_ref, q_ref, qd_ref, kd_ref, vd_ref, w_ref,
    normed_ref, out_ref, held_ref, served_ref,
):
    step = pl.program_id(0)
    heads = held_ref.shape[0]
    tokens = q_ref.shape[0]
    own = place_ref[0]
    mate = partner_ref[own]
    prefill_slot = slot_ref[0]
    length = len_ref[0]
    entries = ids_ref.shape[1]

    def moved(slot):
        memory = states_ref[slot, 0]
        for entry in range(entries):
            leaves = (ids_ref[own, entry] == slot) & (entry < count_ref[own])
            memory = jnp.where(leaves, 0.0, memory)
        for entry in range(entries):
            lands = (ids_ref[mate, entry] == slot) & (entry < count_ref[mate])
            memory = jnp.where(lands, payload_ref[entry, 0].astype(jnp.float32), memory)
        return memory

    @pl.when(step < heads)
    def _():
        slope = slopes_ref[step]
        start = moved(prefill_slot)
        rows = lax.broadcasted_iota(jnp.int32, (tokens, DK), 0)
        leading = jnp.exp(-slope * (rows + 1).astype(jnp.float32))
        attended = att_ref[...] + leading * split_dot(q_ref[...], start)
        normed = jnp.where(rows < length, head_norm(attended), 0.0).astype(jnp.bfloat16)
        held_ref[step, :tokens, :] = normed
        normed_ref[:tokens, :] = normed

        fade = jnp.exp(jnp.full((1, DK), -slope * length.astype(jnp.float32)))
        keep = jnp.exp(jnp.full((1, DK), -slope))
        final = fade * start + mem_ref[0]
        slots = decode_ref.shape[1]
        first_rows, second_rows = [], []
        q_all = qd_ref[...].astype(jnp.float32)
        k_all = kd_ref[...].astype(jnp.float32)
        v_all = vd_ref[...].astype(jnp.float32)
        for row in range(slots):
            slot = decode_ref[0, row]
            memory = jnp.where(slot == prefill_slot, final, moved(slot))
            query = qd_ref[:, row, :]
            seen = split_dot(jnp.concatenate([query] * 8, axis=0), memory)
            q_now, k_now, v_now = q_all[:, row], k_all[:, row], v_all[:, row]
            pair = lambda e, f: jnp.sum(q_now[e : e + 1] * k_now[f : f + 1], axis=-1, keepdims=True)
            first = keep * seen[0:1] + pair(0, 0) * v_now[0:1]
            second = (
                keep * (keep * seen[1:2] + pair(1, 0) * v_now[0:1]) + pair(1, 1) * v_now[1:2]
            )
            first_rows.append(first)
            second_rows.append(second)
        decoded = head_norm(jnp.concatenate(first_rows + second_rows, axis=0))
        padding = jnp.zeros((PAD - decoded.shape[0], DK), jnp.float32)
        decoded = jnp.concatenate([decoded, padding], axis=0).astype(jnp.bfloat16)
        held_ref[step, tokens:, :] = decoded
        normed_ref[tokens:, :] = decoded

    @pl.when(step >= heads)
    def _():
        total = dot(held_ref[0], w_ref[:DK, :])
        for head in range(1, heads):
            total += dot(held_ref[head], w_ref[head * DK : (head + 1) * DK, :])
        out_ref[0] = total.astype(jnp.bfloat16)


def far_chip(place, step):
    return lax.rem(place[1] // 2 + jnp.where(step == 0, ORDER[0], jnp.where(step == 1, ORDER[1], jnp.where(step == 2, ORDER[2], ORDER[3]))), 4)


def serve(place, scalars, states, payload, attended, memory, q_prefill, decode, w_out):
    slots, heads = states.shape[:2]
    tokens, width = q_prefill.shape
    cols = w_out.shape[1] // 8
    steps = decode[0].shape[0]
    rows = tokens + PAD
    at = lambda s: jnp.minimum(s, heads - 1)
    dest = lambda s: jnp.maximum(s - heads, 0)
    column = pl.BlockSpec((tokens, DK), lambda s, *_: (0, at(s)))
    row = pl.BlockSpec((steps, slots, DK), lambda s, *_: (0, 0, at(s)))
    w_block = pl.BlockSpec(
        (width, cols),
        lambda s, place, *_: (0, 2 * far_chip(place, dest(s)) + 1 - lax.rem(place[1], 2)),
    )
    return pl.pallas_call(
        serve_kernel,
        out_shape=(
            jax.ShapeDtypeStruct((rows, width), jnp.bfloat16),
            jax.ShapeDtypeStruct((4, rows, cols), jnp.bfloat16),
        ),
        grid_spec=pltpu.PrefetchScalarGridSpec(
            num_scalar_prefetch=8,
            grid=(heads + 4,),
            in_specs=[
                pl.BlockSpec((slots, 1, DK, DK), lambda s, *_: (0, at(s), 0, 0)),
                pl.BlockSpec((payload.shape[0], 1, DK, DK), lambda s, *_: (0, at(s), 0, 0)),
                column,
                pl.BlockSpec((1, DK, DK), lambda s, *_: (at(s), 0, 0)),
                column,
                row,
                row,
                row,
                w_block,
            ],
            out_specs=(
                pl.BlockSpec((rows, DK), lambda s, *_: (0, at(s))),
                pl.BlockSpec((1, rows, cols), lambda s, *_: (dest(s), 0, 0)),
            ),
            scratch_shapes=[
                pltpu.VMEM((heads, rows, DK), jnp.bfloat16),
                pltpu.VMEM((8, DK), jnp.float32),
            ],
        ),
        compiler_params=params(),
        name="serve",
    )(place, *scalars, states, payload, attended, memory, q_prefill, *decode, w_out)


def join_kernel(place_ref, normed_ref, w_ref, other_ref, *out_refs):
    step = pl.program_id(0)
    total = dot(normed_ref[...], w_ref[...]) + other_ref[0].astype(jnp.float32)
    rounded = total.astype(jnp.bfloat16)
    for index, out_ref in enumerate(out_refs):

        @pl.when(step == index)
        def _():
            out_ref[...] = rounded


def join(place, normed, w_out, other):
    rows, width = normed.shape
    cols = w_out.shape[1] // 8
    return pl.pallas_call(
        join_kernel,
        out_shape=(jax.ShapeDtypeStruct((rows, cols), jnp.bfloat16),) * 4,
        grid_spec=pltpu.PrefetchScalarGridSpec(
            num_scalar_prefetch=1,
            grid=(4,),
            in_specs=[
                pl.BlockSpec((rows, width), lambda s, *_: (0, 0)),
                pl.BlockSpec(
                    (width, cols),
                    lambda s, place: (0, 2 * far_chip(place, s) + lax.rem(place[1], 2)),
                ),
                pl.BlockSpec((1, rows, cols), lambda s, *_: (s, 0, 0)),
            ],
            out_specs=(pl.BlockSpec((rows, cols), lambda s, *_: (0, 0)),) * 4,
        ),
        compiler_params=params(),
        name="join",
    )(place, normed, w_out, other)


def finish_kernel(a_ref, b_ref, c_ref, d_ref, prefill_ref, decode_ref):
    total = a_ref[...].astype(jnp.float32) + b_ref[...].astype(jnp.float32)
    total += c_ref[...].astype(jnp.float32)
    total += d_ref[...].astype(jnp.float32)
    rounded = total.astype(jnp.bfloat16)
    tokens = prefill_ref.shape[0]
    prefill_ref[...] = rounded[:tokens]
    steps, slots, _ = decode_ref.shape
    for step in range(steps):
        first = tokens + step * slots
        decode_ref[step] = total[first : first + slots].astype(jnp.bfloat16)


def finish(parts, tokens, steps, slots):
    cols = parts[0].shape[1]
    return pl.pallas_call(
        finish_kernel,
        out_shape=(
            jax.ShapeDtypeStruct((tokens, cols), jnp.bfloat16),
            jax.ShapeDtypeStruct((steps, slots, cols), jnp.bfloat16),
        ),
        compiler_params=params(0),
        name="finish",
    )(*parts)


def exchange(array, pattern):
    size = lax.axis_size("replica")
    return lax.ppermute(array, "replica", [(i, i ^ pattern) for i in range(size)])


def on_device(
    states,
    partner,
    send_ids,
    send_count,
    prefill_slot,
    prompt_len,
    decode_slots,
    q_prefill,
    k_prefill,
    v_prefill,
    q_decode,
    k_decode,
    v_decode,
    slopes,
    w_out,
):
    size = lax.axis_size("replica")
    own = lax.axis_index("replica")
    head = lax.axis_index("head")
    place = jnp.stack([own, head]).astype(jnp.int32)
    payload = pack(place, send_ids, states)

    half, across = size // 2, size // 4 * 3

    def branch(pattern, payload, *prefill):
        moving = payload
        if pattern >= half:
            moving = exchange(moving, across)
            pattern ^= across
        if pattern:
            moving = exchange(moving, pattern)
        return moving, *intra(*prefill)

    payload, attended, memory = lax.switch(
        jnp.clip(partner[0] - 1, 0, size - 2),
        [partial(branch, pattern) for pattern in range(1, size)],
        payload,
        prompt_len,
        slopes,
        q_prefill,
        k_prefill,
        v_prefill,
    )
    scalars = (partner, send_ids, send_count, prefill_slot, prompt_len, decode_slots, slopes)
    normed, other = serve(
        place, scalars, states, payload, attended, memory, q_prefill,
        (q_decode, k_decode, v_decode), w_out,
    )
    devices = lax.axis_size("head")
    other = lax.ppermute(other, "head", [(i, i ^ 1) for i in range(devices)])
    parts = join(place, normed, w_out, other)
    arrived = [
        lax.ppermute(part, "head", [(i, (i + 2 * away) % devices) for i in range(devices)])
        if away
        else part
        for away, part in zip(ORDER, parts, strict=True)
    ]
    steps, slots = q_decode.shape[:2]
    return finish(arrived, q_prefill.shape[0], steps, slots)


def solution(mesh):
    return jax.shard_map(
        on_device,
        mesh=mesh,
        in_specs=(
            P("replica", "head", None, None),
            P(),
            P(),
            P(),
            P("replica"),
            P("replica"),
            P("replica", None),
            P("replica", "head"),
            P("replica", "head"),
            P("replica", "head"),
            P(None, "replica", "head"),
            P(None, "replica", "head"),
            P(None, "replica", "head"),
            P("head"),
            P("head", None),
        ),
        out_specs=(P("replica", "head"), P(None, "replica", "head")),
        check_vma=False,
    )
```

```python
from functools import partial

import jax
import jax.numpy as jnp
from jax import lax
from jax.experimental import pallas as pl
from jax.experimental.pallas import tpu as pltpu
from jax.sharding import PartitionSpec as P

DK = 128
BLK = 128
EPS = 1e-06
PAD = 16
VMEM_LIMIT = 48 * 1024 * 1024
ORDER = (2, 1, 3, 0)


def params(axes=1):
    return pltpu.CompilerParams(
        dimension_semantics=("arbitrary",) * axes, vmem_limit_bytes=VMEM_LIMIT
    )


def dot(left, right, left_dim=1, right_dim=0):
    return lax.dot_general(
        left, right, (((left_dim,), (right_dim,)), ((), ())), preferred_element_type=jnp.float32
    )


def split_dot(left, right):
    high = right.astype(jnp.bfloat16)
    low = (right - high.astype(jnp.float32)).astype(jnp.bfloat16)
    return dot(left, high) + dot(left, low)


def pack_kernel(own_ref, ids_ref, states_ref, out_ref):
    out_ref[...] = states_ref[...].astype(jnp.bfloat16)


def pack(own, send_ids, states):
    _, heads, rows, cols = states.shape
    count = send_ids.shape[0]
    block = (1, heads, rows, cols)
    return pl.pallas_call(
        pack_kernel,
        out_shape=jax.ShapeDtypeStruct((count, heads, rows, cols), jnp.bfloat16),
        grid_spec=pltpu.PrefetchScalarGridSpec(
            num_scalar_prefetch=2,
            grid=(count,),
            in_specs=[pl.BlockSpec(block, lambda j, own, ids: (ids[j, own[0]], 0, 0, 0))],
            out_specs=pl.BlockSpec(block, lambda j, own, ids: (j, 0, 0, 0)),
        ),
        compiler_params=params(),
        name="pack",
    )(own, send_ids, states)


def head_norm(inputs):
    return inputs * lax.rsqrt(jnp.mean(inputs * inputs, axis=-1, keepdims=True) + EPS)


def fade_row(exponent):
    return jnp.exp(jnp.full((1, DK), exponent))


def decode_rows(ref):
    return jnp.concatenate([ref[step].astype(jnp.float32) for step in range(ref.shape[0])], axis=0)


def own_kernel(
    place_ref, partner_ref, ids_ref, count_ref, slot_ref, len_ref, decode_ref, slopes_ref,
    states_ref, q_ref, k_ref, v_ref, qd_ref, kd_ref, vd_ref, mine_ref, theirs_ref,
    att_ref, dec_ref, mine_out_ref, theirs_out_ref, mem_ref,
):
    mine_out_ref[0] = mine_ref[...]
    theirs_out_ref[0] = theirs_ref[...]
    slope = slopes_ref[pl.program_id(0)]
    own = place_ref[0]
    mate = partner_ref[own]
    length = len_ref[0]
    prefill_slot = slot_ref[0]

    def kept(slot):
        gone = jnp.bool_(False)
        for entry in range(ids_ref.shape[0]):
            gone |= (ids_ref[entry, own] == slot) & (entry < count_ref[own])
            gone |= (ids_ref[entry, mate] == slot) & (entry < count_ref[mate])
        return jnp.where(gone, 0.0, states_ref[slot, 0])

    rows = lax.broadcasted_iota(jnp.int32, (BLK, BLK), 0)
    cols = lax.broadcasted_iota(jnp.int32, (BLK, BLK), 1)
    damping = jnp.exp(-slope * jnp.maximum(rows - cols, 0).astype(jnp.float32))
    leading = jnp.exp(-slope * (rows + 1).astype(jnp.float32))
    mem_ref[...] = kept(prefill_slot)

    def step(block, carry):
        count = jnp.clip(length - block * BLK, 0, BLK)
        here = pl.ds(pl.multiple_of(block * BLK, BLK), BLK)
        q_block, k_block, v_block = q_ref[here, :], k_ref[here, :], v_ref[here, :]
        memory = mem_ref[...]
        scores = dot(q_block, k_block, 1, 1)
        valid = (cols <= rows) & (cols < count)
        probs = jnp.where(valid, scores * damping, 0.0).astype(jnp.bfloat16)
        att_ref[here, :] = dot(probs, v_block) + leading * split_dot(q_block, memory)
        behind = jnp.maximum(count - 1 - rows, 0).astype(jnp.float32)
        trailing = jnp.where(rows < count, jnp.exp(-slope * behind), 0.0)
        weighted = (k_block.astype(jnp.float32) * trailing).astype(jnp.bfloat16)
        mem_ref[...] = fade_row(-slope * count.astype(jnp.float32)) * memory + dot(
            weighted, v_block, 0, 0
        )
        return carry

    lax.fori_loop(0, q_ref.shape[0] // BLK, step, 0)

    keep = fade_row(-slope)
    slots = decode_ref.shape[1]
    queries, keys, values = (decode_rows(ref) for ref in (qd_ref, kd_ref, vd_ref))
    padded = jnp.concatenate([queries, queries], axis=0).astype(jnp.bfloat16)
    place = lax.broadcasted_iota(jnp.int32, (2 * slots, DK), 0)
    seen = jnp.zeros((2 * slots, DK), jnp.float32)
    for row in range(slots):
        slot = decode_ref[0, row]
        memory = jnp.where(slot == prefill_slot, mem_ref[...], kept(slot))
        seen = jnp.where(place % slots == row, split_dot(padded, memory)[: 2 * slots], seen)
    product = lambda q, k: jnp.sum(q * k, axis=-1, keepdims=True)
    first, second = slice(0, slots), slice(slots, 2 * slots)
    now = product(queries, keys) * values
    before = product(queries[second], keys[first]) * values[first]
    dec_ref[first, :] = keep * seen[first] + now[first]
    dec_ref[second, :] = keep * (keep * seen[second] + before) + now[second]


def far_chip(place, step):
    away = jnp.where(
        step == 0, ORDER[0], jnp.where(step == 1, ORDER[1], jnp.where(step == 2, ORDER[2], ORDER[3]))
    )
    return lax.rem(place[1] // 2 + away, 4)


def own_part(place, scalars, states, prefill, decode, w_out):
    slots, heads = states.shape[:2]
    tokens, width = prefill[0].shape
    cols = w_out.shape[1] // 8
    steps = decode[0].shape[0]
    column = pl.BlockSpec((tokens, DK), lambda h, *_: (0, h))
    row = pl.BlockSpec((steps, slots, DK), lambda h, *_: (0, 0, h))
    taken = pl.BlockSpec((1, width, cols), lambda h, *_: (h, 0, 0))

    def weights(other):
        def index(h, place, *_):
            core = lax.rem(place[1], 2)
            return (0, 2 * far_chip(place, h) + (1 - core if other else core))

        return pl.BlockSpec((width, cols), index)

    return pl.pallas_call(
        own_kernel,
        out_shape=(
            jax.ShapeDtypeStruct((tokens, width), jnp.float32),
            jax.ShapeDtypeStruct((steps * slots, width), jnp.float32),
            jax.ShapeDtypeStruct((4, width, cols), jnp.bfloat16),
            jax.ShapeDtypeStruct((4, width, cols), jnp.bfloat16),
        ),
        grid_spec=pltpu.PrefetchScalarGridSpec(
            num_scalar_prefetch=8,
            grid=(heads,),
            in_specs=[
                pl.BlockSpec((slots, 1, DK, DK), lambda h, *_: (0, h, 0, 0)),
                column,
                column,
                column,
                row,
                row,
                row,
                weights(False),
                weights(True),
            ],
            out_specs=(
                column,
                pl.BlockSpec((steps * slots, DK), lambda h, *_: (0, h)),
                taken,
                taken,
            ),
            scratch_shapes=[pltpu.VMEM((DK, DK), jnp.float32)],
        ),
        compiler_params=params(),
        cost_estimate=pl.CostEstimate(
            flops=10 * tokens * BLK * width,
            bytes_accessed=5 * tokens * width * 2 + 4 * w_out.size,
            transcendentals=0,
        ),
        name="own_part",
    )(place, *scalars, states, *prefill, *decode, w_out, w_out)


def serve_kernel(
    place_ref, partner_ref, ids_ref, count_ref, slot_ref, len_ref, decode_ref, slopes_ref,
    payload_ref, att_ref, dec_ref, q_ref, qd_ref, normed_ref,
):
    tokens, width = q_ref.shape
    mate = partner_ref[place_ref[0]]
    prefill_slot = slot_ref[0]
    length = len_ref[0]
    slots = decode_ref.shape[1]
    entries = ids_ref.shape[0]
    lands = [
        lambda slot, e=e: ((ids_ref[e, mate] == slot) & (e < count_ref[mate])) for e in range(entries)
    ]
    rows = lax.broadcasted_iota(jnp.int32, (tokens, DK), 0)
    place = lax.broadcasted_iota(jnp.int32, (2 * slots, DK), 0)
    later = (rows + 1).astype(jnp.float32)
    is_valid = rows < length
    for head in range(width // DK):
        here = slice(head * DK, (head + 1) * DK)
        slope = slopes_ref[head]
        chosen = jnp.zeros((DK, DK), jnp.bfloat16)
        for entry in range(entries):
            chosen = jnp.where(lands[entry](prefill_slot), payload_ref[entry, head], chosen)
        attended = att_ref[:, here] + jnp.exp(-slope * later) * dot(q_ref[:, here], chosen)
        normed = jnp.where(is_valid, head_norm(attended), 0.0)
        normed_ref[:tokens, here] = normed.astype(jnp.bfloat16)

        keep = fade_row(-slope)
        faded = fade_row(-slope * length.astype(jnp.float32))
        queries = decode_rows(qd_ref.at[:, :, here])
        padded = jnp.concatenate([queries, queries], axis=0).astype(jnp.bfloat16)
        scale = jnp.where(place < slots, keep, keep * keep)
        decoded = dec_ref[:, here]
        for entry in range(entries):
            seen = dot(padded, payload_ref[entry, head])[: 2 * slots]
            share = jnp.zeros((2 * slots, DK), jnp.float32)
            for row in range(slots):
                slot = decode_ref[0, row]
                factor = jnp.where(slot == prefill_slot, faded, 1.0)
                factor = jnp.where(lands[entry](slot), factor, 0.0)
                share = jnp.where(place % slots == row, factor, share)
            decoded += scale * share * seen
        decoded = head_norm(decoded)
        padding = jnp.zeros((PAD - 2 * slots, DK), jnp.float32)
        decoded = jnp.concatenate([decoded, padding], axis=0)
        normed_ref[tokens:, here] = decoded.astype(jnp.bfloat16)


def serve(place, scalars, payload, attended, decoded, q_prefill, q_decode):
    tokens, width = q_prefill.shape
    scalar = pl.BlockSpec(memory_space=pltpu.SMEM)
    whole = pl.BlockSpec(memory_space=pltpu.VMEM)
    return pl.pallas_call(
        serve_kernel,
        out_shape=jax.ShapeDtypeStruct((tokens + PAD, width), jnp.bfloat16),
        in_specs=[scalar] * 8 + [whole] * 5,
        out_specs=whole,
        compiler_params=params(0),
        name="serve",
    )(place, *scalars, payload, attended, decoded, q_prefill, q_decode)


def join_kernel(first, own_ref, other_ref, mine_ref, theirs_ref, *out_refs):
    for index, out_ref in enumerate(out_refs):
        total = dot(own_ref[...], mine_ref[first + index])
        total += dot(other_ref[...], theirs_ref[first + index])
        out_ref[...] = total.astype(jnp.bfloat16)


def join(own, other, mine, theirs, first, count):
    whole = pl.BlockSpec(memory_space=pltpu.VMEM)
    shape = (own.shape[0], mine.shape[2])
    return pl.pallas_call(
        partial(join_kernel, first),
        out_shape=(jax.ShapeDtypeStruct(shape, jnp.bfloat16),) * count,
        in_specs=[whole] * 4,
        out_specs=(whole,) * count,
        compiler_params=params(0),
        name=f"join{first}",
        cost_estimate=pl.CostEstimate(
            flops=4 * count * own.size * mine.shape[2],
            bytes_accessed=4 * own.size + 4 * count * mine.shape[1] * mine.shape[2],
            transcendentals=0,
        ),
    )(own, other, mine, theirs)


def finish_kernel(a_ref, b_ref, c_ref, d_ref, prefill_ref, decode_ref):
    total = a_ref[...].astype(jnp.float32) + b_ref[...].astype(jnp.float32)
    total += c_ref[...].astype(jnp.float32)
    total += d_ref[...].astype(jnp.float32)
    rounded = total.astype(jnp.bfloat16)
    tokens = prefill_ref.shape[0]
    prefill_ref[...] = rounded[:tokens]
    steps, slots, _ = decode_ref.shape
    for step in range(steps):
        first = tokens + step * slots
        decode_ref[step] = total[first : first + slots].astype(jnp.bfloat16)


def finish(parts, tokens, steps, slots):
    cols = parts[0].shape[1]
    return pl.pallas_call(
        finish_kernel,
        out_shape=(
            jax.ShapeDtypeStruct((tokens, cols), jnp.bfloat16),
            jax.ShapeDtypeStruct((steps, slots, cols), jnp.bfloat16),
        ),
        compiler_params=params(0),
        name="finish",
    )(*parts)


def as_one(partner, step, *arrays):
    def nothing(*arrays):
        return jax.tree.map(lambda a: jnp.zeros(a.shape, a.dtype), jax.eval_shape(step, *arrays))

    return lax.cond(partner[0] >= 0, step, nothing, *arrays)


def exchange(array, pattern):
    size = lax.axis_size("replica")
    return lax.ppermute(array, "replica", [(i, i ^ pattern) for i in range(size)])


def on_device(
    states,
    partner,
    send_ids,
    send_count,
    prefill_slot,
    prompt_len,
    decode_slots,
    q_prefill,
    k_prefill,
    v_prefill,
    q_decode,
    k_decode,
    v_decode,
    slopes,
    w_out,
):
    size = lax.axis_size("replica")
    own = lax.axis_index("replica")
    head = lax.axis_index("head")
    place = jnp.stack([own, head]).astype(jnp.int32)
    ids = send_ids.T
    payload = pack(place, ids, states)
    scalars = (partner, ids, send_count, prefill_slot, prompt_len, decode_slots, slopes)
    devices = lax.axis_size("head")
    siblings = [(i, i ^ 1) for i in range(devices)]

    half, across = size // 2, size // 4 * 3

    def local(*arrays):
        attended, decoded, mine, theirs = own_part(*arrays)
        return attended, decoded, mine, lax.ppermute(theirs, "head", siblings)

    def branch(pattern, payload, *arrays):
        moving = payload
        if pattern >= half:
            moving = exchange(moving, across)
            pattern ^= across
        if pattern:
            moving = exchange(moving, pattern)
        return moving, *as_one(partner, local, *arrays)

    payload, attended, decoded, mine, theirs = lax.switch(
        jnp.clip(partner[0] - 1, 0, size - 2),
        [partial(branch, pattern) for pattern in range(1, size)],
        payload,
        place,
        scalars,
        states,
        (q_prefill, k_prefill, v_prefill),
        (q_decode, k_decode, v_decode),
        w_out,
    )
    normed = serve(place, scalars, payload, attended, decoded, q_prefill, q_decode)
    other = lax.ppermute(normed, "head", siblings)

    def along(part, away):
        return lax.ppermute(part, "head", [(i, (i + 2 * away) % devices) for i in range(devices)])

    def nearer(*arrays):
        *near, here = join(*arrays, 1, 3)
        return *(along(part, away) for part, away in zip(near, ORDER[1:-1], strict=True)), here

    (farthest,) = join(normed, other, mine, theirs, 0, 1)
    farthest, normed = lax.optimization_barrier((farthest, normed))
    farthest = along(farthest, ORDER[0])
    arrived = (farthest, *as_one(partner, nearer, normed, other, mine, theirs))
    steps, slots = q_decode.shape[:2]
    return finish(arrived, q_prefill.shape[0], steps, slots)


def solution(mesh):
    return jax.shard_map(
        on_device,
        mesh=mesh,
        in_specs=(
            P("replica", "head", None, None),
            P(),
            P(),
            P(),
            P("replica"),
            P("replica"),
            P("replica", None),
            P("replica", "head"),
            P("replica", "head"),
            P("replica", "head"),
            P(None, "replica", "head"),
            P(None, "replica", "head"),
            P(None, "replica", "head"),
            P("head"),
            P("head", None),
        ),
        out_specs=(P("replica", "head"), P(None, "replica", "head")),
        check_vma=False,
    )
```

```python
from functools import partial

import jax
import jax.numpy as jnp
from jax import lax
from jax.experimental import pallas as pl
from jax.experimental.pallas import tpu as pltpu
from jax.sharding import PartitionSpec as P

DK = 128
BLK = 128
EPS = 1e-06
PAD = 16
VMEM_LIMIT = 48 * 1024 * 1024
ORDER = (2, 1, 3, 0)


def params(axes=1):
    return pltpu.CompilerParams(
        dimension_semantics=("arbitrary",) * axes, vmem_limit_bytes=VMEM_LIMIT
    )


def dot(left, right, left_dim=1, right_dim=0):
    return lax.dot_general(
        left, right, (((left_dim,), (right_dim,)), ((), ())), preferred_element_type=jnp.float32
    )


def split_dot(left, right):
    high = right.astype(jnp.bfloat16)
    low = (right - high.astype(jnp.float32)).astype(jnp.bfloat16)
    return dot(left, high) + dot(left, low)


def pack_kernel(own_ref, ids_ref, states_ref, out_ref):
    out_ref[...] = states_ref[...].astype(jnp.bfloat16)


def pack(own, send_ids, states):
    _, heads, rows, cols = states.shape
    count = send_ids.shape[0]
    block = (1, heads, rows, cols)
    return pl.pallas_call(
        pack_kernel,
        out_shape=jax.ShapeDtypeStruct((count, heads, rows, cols), jnp.bfloat16),
        grid_spec=pltpu.PrefetchScalarGridSpec(
            num_scalar_prefetch=2,
            grid=(count,),
            in_specs=[pl.BlockSpec(block, lambda j, own, ids: (ids[j, own[0]], 0, 0, 0))],
            out_specs=pl.BlockSpec(block, lambda j, own, ids: (j, 0, 0, 0)),
        ),
        compiler_params=params(),
        name="pack",
    )(own, send_ids, states)


def copy_kernel(in_ref, out_ref):
    out_ref[...] = in_ref[...]


def copied(array):
    return pl.pallas_call(
        copy_kernel,
        out_shape=jax.ShapeDtypeStruct(array.shape, array.dtype),
        compiler_params=params(0),
        name="copied",
    )(array)


def head_norm(inputs):
    return inputs * lax.rsqrt(jnp.mean(inputs * inputs, axis=-1, keepdims=True) + EPS)


def fade_row(exponent):
    return jnp.exp(jnp.full((1, DK), exponent))


def decode_rows(ref):
    return jnp.concatenate([ref[step].astype(jnp.float32) for step in range(ref.shape[0])], axis=0)


def own_kernel(
    place_ref, partner_ref, ids_ref, count_ref, slot_ref, len_ref, decode_ref, slopes_ref,
    states_ref, q_ref, k_ref, v_ref, qd_ref, kd_ref, vd_ref, mine_ref, theirs_ref,
    att_ref, dec_ref, mine_out_ref, theirs_out_ref, mem_ref,
):
    mine_out_ref[0] = mine_ref[...]
    theirs_out_ref[0] = theirs_ref[...]
    slope = slopes_ref[pl.program_id(0)]
    own = place_ref[0]
    mate = partner_ref[own]
    length = len_ref[0]
    prefill_slot = slot_ref[0]

    def kept(slot):
        gone = jnp.bool_(False)
        for entry in range(ids_ref.shape[0]):
            gone |= (ids_ref[entry, own] == slot) & (entry < count_ref[own])
            gone |= (ids_ref[entry, mate] == slot) & (entry < count_ref[mate])
        return jnp.where(gone, 0.0, states_ref[slot, 0])

    rows = lax.broadcasted_iota(jnp.int32, (BLK, BLK), 0)
    cols = lax.broadcasted_iota(jnp.int32, (BLK, BLK), 1)
    damping = jnp.exp(-slope * jnp.maximum(rows - cols, 0).astype(jnp.float32))
    leading = jnp.exp(-slope * (rows + 1).astype(jnp.float32))
    mem_ref[...] = kept(prefill_slot)

    def step(block, carry):
        count = jnp.clip(length - block * BLK, 0, BLK)
        here = pl.ds(pl.multiple_of(block * BLK, BLK), BLK)
        q_block, k_block, v_block = q_ref[here, :], k_ref[here, :], v_ref[here, :]
        memory = mem_ref[...]
        scores = dot(q_block, k_block, 1, 1)
        valid = (cols <= rows) & (cols < count)
        probs = jnp.where(valid, scores * damping, 0.0).astype(jnp.bfloat16)
        att_ref[here, :] = dot(probs, v_block) + leading * split_dot(q_block, memory)
        behind = jnp.maximum(count - 1 - rows, 0).astype(jnp.float32)
        trailing = jnp.where(rows < count, jnp.exp(-slope * behind), 0.0)
        weighted = (k_block.astype(jnp.float32) * trailing).astype(jnp.bfloat16)
        mem_ref[...] = fade_row(-slope * count.astype(jnp.float32)) * memory + dot(
            weighted, v_block, 0, 0
        )
        return carry

    lax.fori_loop(0, q_ref.shape[0] // BLK, step, 0)

    keep = fade_row(-slope)
    slots = decode_ref.shape[1]
    queries, keys, values = (decode_rows(ref) for ref in (qd_ref, kd_ref, vd_ref))
    padded = jnp.concatenate([queries, queries], axis=0).astype(jnp.bfloat16)
    place = lax.broadcasted_iota(jnp.int32, (2 * slots, DK), 0)
    seen = jnp.zeros((2 * slots, DK), jnp.float32)
    for row in range(slots):
        slot = decode_ref[0, row]
        memory = jnp.where(slot == prefill_slot, mem_ref[...], kept(slot))
        seen = jnp.where(place % slots == row, split_dot(padded, memory)[: 2 * slots], seen)
    product = lambda q, k: jnp.sum(q * k, axis=-1, keepdims=True)
    first, second = slice(0, slots), slice(slots, 2 * slots)
    now = product(queries, keys) * values
    before = product(queries[second], keys[first]) * values[first]
    dec_ref[first, :] = keep * seen[first] + now[first]
    dec_ref[second, :] = keep * (keep * seen[second] + before) + now[second]


def far_chip(place, step):
    away = jnp.where(
        step == 0, ORDER[0], jnp.where(step == 1, ORDER[1], jnp.where(step == 2, ORDER[2], ORDER[3]))
    )
    return lax.rem(place[1] // 2 + away, 4)


def own_part(place, scalars, states, prefill, decode, w_out):
    slots, heads = states.shape[:2]
    tokens, width = prefill[0].shape
    cols = w_out.shape[1] // 8
    steps = decode[0].shape[0]
    column = pl.BlockSpec((tokens, DK), lambda h, *_: (0, h))
    row = pl.BlockSpec((steps, slots, DK), lambda h, *_: (0, 0, h))
    taken = pl.BlockSpec((1, width, cols), lambda h, *_: (h, 0, 0))

    def weights(other):
        def index(h, place, *_):
            core = lax.rem(place[1], 2)
            return (0, 2 * far_chip(place, h) + (1 - core if other else core))

        return pl.BlockSpec((width, cols), index)

    return pl.pallas_call(
        own_kernel,
        out_shape=(
            jax.ShapeDtypeStruct((tokens, width), jnp.float32),
            jax.ShapeDtypeStruct((steps * slots, width), jnp.float32),
            jax.ShapeDtypeStruct((4, width, cols), jnp.bfloat16),
            jax.ShapeDtypeStruct((4, width, cols), jnp.bfloat16),
        ),
        grid_spec=pltpu.PrefetchScalarGridSpec(
            num_scalar_prefetch=8,
            grid=(heads,),
            in_specs=[
                pl.BlockSpec((slots, 1, DK, DK), lambda h, *_: (0, h, 0, 0)),
                column,
                column,
                column,
                row,
                row,
                row,
                weights(False),
                weights(True),
            ],
            out_specs=(
                column,
                pl.BlockSpec((steps * slots, DK), lambda h, *_: (0, h)),
                taken,
                taken,
            ),
            scratch_shapes=[pltpu.VMEM((DK, DK), jnp.float32)],
        ),
        compiler_params=params(),
        cost_estimate=pl.CostEstimate(
            flops=10 * tokens * BLK * width,
            bytes_accessed=5 * tokens * width * 2 + 4 * w_out.size,
            transcendentals=0,
        ),
        name="own_part",
    )(place, *scalars, states, *prefill, *decode, w_out, w_out)


def serve_kernel(
    place_ref, partner_ref, ids_ref, count_ref, slot_ref, len_ref, decode_ref, slopes_ref,
    payload_ref, att_ref, dec_ref, q_ref, qd_ref, normed_ref,
):
    tokens, width = q_ref.shape
    mate = partner_ref[place_ref[0]]
    prefill_slot = slot_ref[0]
    length = len_ref[0]
    slots = decode_ref.shape[1]
    entries = ids_ref.shape[0]
    lands = [
        lambda slot, e=e: ((ids_ref[e, mate] == slot) & (e < count_ref[mate])) for e in range(entries)
    ]
    rows = lax.broadcasted_iota(jnp.int32, (tokens, DK), 0)
    place = lax.broadcasted_iota(jnp.int32, (2 * slots, DK), 0)
    later = (rows + 1).astype(jnp.float32)
    is_valid = rows < length
    for head in range(width // DK):
        here = slice(head * DK, (head + 1) * DK)
        slope = slopes_ref[head]
        chosen = jnp.zeros((DK, DK), jnp.bfloat16)
        for entry in range(entries):
            chosen = jnp.where(lands[entry](prefill_slot), payload_ref[entry, head], chosen)
        attended = att_ref[:, here] + jnp.exp(-slope * later) * dot(q_ref[:, here], chosen)
        normed = jnp.where(is_valid, head_norm(attended), 0.0)
        normed_ref[:tokens, here] = normed.astype(jnp.bfloat16)

        keep = fade_row(-slope)
        faded = fade_row(-slope * length.astype(jnp.float32))
        queries = decode_rows(qd_ref.at[:, :, here])
        padded = jnp.concatenate([queries, queries], axis=0).astype(jnp.bfloat16)
        scale = jnp.where(place < slots, keep, keep * keep)
        decoded = dec_ref[:, here]
        for entry in range(entries):
            seen = dot(padded, payload_ref[entry, head])[: 2 * slots]
            share = jnp.zeros((2 * slots, DK), jnp.float32)
            for row in range(slots):
                slot = decode_ref[0, row]
                factor = jnp.where(slot == prefill_slot, faded, 1.0)
                factor = jnp.where(lands[entry](slot), factor, 0.0)
                share = jnp.where(place % slots == row, factor, share)
            decoded += scale * share * seen
        decoded = head_norm(decoded)
        padding = jnp.zeros((PAD - 2 * slots, DK), jnp.float32)
        decoded = jnp.concatenate([decoded, padding], axis=0)
        normed_ref[tokens:, here] = decoded.astype(jnp.bfloat16)


def serve(place, scalars, payload, attended, decoded, q_prefill, q_decode):
    tokens, width = q_prefill.shape
    scalar = pl.BlockSpec(memory_space=pltpu.SMEM)
    whole = pl.BlockSpec(memory_space=pltpu.VMEM)
    return pl.pallas_call(
        serve_kernel,
        out_shape=jax.ShapeDtypeStruct((tokens + PAD, width), jnp.bfloat16),
        in_specs=[scalar] * 8 + [whole] * 5,
        out_specs=whole,
        compiler_params=params(0),
        name="serve",
    )(place, *scalars, payload, attended, decoded, q_prefill, q_decode)


def join_kernel(own_ref, other_ref, *refs):
    count = len(refs) // 3
    for mine_ref, theirs_ref, out_ref in zip(refs[:count], refs[count : 2 * count], refs[2 * count :]):
        total = dot(own_ref[...], mine_ref[0]) + dot(other_ref[...], theirs_ref[0])
        out_ref[...] = total.astype(jnp.bfloat16)


def join(own, other, mine, theirs, chips):
    whole = pl.BlockSpec(memory_space=pltpu.VMEM)
    count = len(chips)
    shape = (own.shape[0], mine.shape[2])
    blocks = [pl.BlockSpec((1, *mine.shape[1:]), lambda i, chip=chip: (chip, 0, 0)) for chip in chips]
    return pl.pallas_call(
        join_kernel,
        out_shape=(jax.ShapeDtypeStruct(shape, jnp.bfloat16),) * count,
        grid=(1,),
        in_specs=[whole] * 2 + blocks * 2,
        out_specs=(whole,) * count,
        compiler_params=params(),
        name=f"join{chips[0]}",
        cost_estimate=pl.CostEstimate(
            flops=4 * count * own.size * mine.shape[2],
            bytes_accessed=4 * own.size + 4 * count * mine.shape[1] * mine.shape[2],
            transcendentals=0,
        ),
    )(own, other, *[mine] * count, *[theirs] * count)


def add_kernel(a_ref, b_ref, out_ref):
    out_ref[...] = a_ref[...].astype(jnp.float32) + b_ref[...].astype(jnp.float32)


def add(a, b):
    return pl.pallas_call(
        add_kernel,
        out_shape=jax.ShapeDtypeStruct(a.shape, jnp.float32),
        compiler_params=params(0),
        name="add",
    )(a, b)


def finish_kernel(a_ref, b_ref, c_ref, prefill_ref, decode_ref):
    total = a_ref[...] + b_ref[...].astype(jnp.float32) + c_ref[...].astype(jnp.float32)
    tokens = prefill_ref.shape[0]
    prefill_ref[...] = total[:tokens].astype(jnp.bfloat16)
    steps, slots, _ = decode_ref.shape
    for step in range(steps):
        first = tokens + step * slots
        decode_ref[step] = total[first : first + slots].astype(jnp.bfloat16)


def finish(total, near, tokens, steps, slots):
    cols = total.shape[1]
    return pl.pallas_call(
        finish_kernel,
        out_shape=(
            jax.ShapeDtypeStruct((tokens, cols), jnp.bfloat16),
            jax.ShapeDtypeStruct((steps, slots, cols), jnp.bfloat16),
        ),
        compiler_params=params(0),
        name="finish",
    )(total, *near)


def siblings():
    return [(i, i ^ 1) for i in range(lax.axis_size("head"))]


def swapped(partner, array):
    return lax.cond(
        partner[0] >= 0, lambda own: lax.ppermute(own, "head", siblings()), jnp.zeros_like, array
    )


def exchange(array, pattern):
    size = lax.axis_size("replica")
    return lax.ppermute(array, "replica", [(i, i ^ pattern) for i in range(size)])


def on_device(
    states,
    partner,
    send_ids,
    send_count,
    prefill_slot,
    prompt_len,
    decode_slots,
    q_prefill,
    k_prefill,
    v_prefill,
    q_decode,
    k_decode,
    v_decode,
    slopes,
    w_out,
):
    size = lax.axis_size("replica")
    own = lax.axis_index("replica")
    head = lax.axis_index("head")
    place = jnp.stack([own, head]).astype(jnp.int32)
    ids = send_ids.T
    scalars = (partner, ids, send_count, prefill_slot, prompt_len, decode_slots, slopes)
    devices = lax.axis_size("head")

    pattern = jnp.clip(partner[0], 1, size - 1)
    half, across = size // 2, size // 4 * 3

    def hop(*arrays):
        return exchange(pack(*arrays), across)

    payload = lax.cond(pattern >= half, hop, pack, place, ids, states)

    def branch(rest, payload, *arrays):
        moving = exchange(payload, rest) if rest else copied(payload)
        attended, decoded, mine, theirs = own_part(*arrays)
        return moving, attended, decoded, mine, swapped(partner, theirs)

    payload, attended, decoded, mine, theirs = lax.switch(
        jnp.where(pattern >= half, pattern ^ across, pattern),
        [partial(branch, rest) for rest in range(half)],
        payload,
        place,
        scalars,
        states,
        (q_prefill, k_prefill, v_prefill),
        (q_decode, k_decode, v_decode),
        w_out,
    )
    normed = serve(place, scalars, payload, attended, decoded, q_prefill, q_decode)
    other = lax.ppermute(normed, "head", siblings())

    def along(part, away):
        return lax.ppermute(part, "head", [(i, (i + 2 * away) % devices) for i in range(devices)])

    (farthest,) = join(normed, other, mine, theirs, (0,))
    farthest, normed = lax.optimization_barrier((farthest, normed))
    *near, here = join(normed, other, mine, theirs, (1, 2, 3))
    near = [along(part, away) for part, away in zip(near, ORDER[1:-1], strict=True)]
    total = add(along(farthest, ORDER[0]), here)
    steps, slots = q_decode.shape[:2]
    return finish(total, near, q_prefill.shape[0], steps, slots)


def solution(mesh):
    return jax.shard_map(
        on_device,
        mesh=mesh,
        in_specs=(
            P("replica", "head", None, None),
            P(),
            P(),
            P(),
            P("replica"),
            P("replica"),
            P("replica", None),
            P("replica", "head"),
            P("replica", "head"),
            P("replica", "head"),
            P(None, "replica", "head"),
            P(None, "replica", "head"),
            P(None, "replica", "head"),
            P("head"),
            P("head", None),
        ),
        out_specs=(P("replica", "head"), P(None, "replica", "head")),
        check_vma=False,
    )
```

```python
from functools import partial

import jax
import jax.numpy as jnp
from jax import lax
from jax.experimental import pallas as pl
from jax.experimental.pallas import tpu as pltpu
from jax.sharding import PartitionSpec as P

DK = 128
BLK = 128
EPS = 1e-06
PAD = 16
VMEM_LIMIT = 48 * 1024 * 1024
ORDER = (2, 1, 3, 0)


def params(axes=1):
    return pltpu.CompilerParams(
        dimension_semantics=("arbitrary",) * axes, vmem_limit_bytes=VMEM_LIMIT
    )


def dot(left, right, left_dim=1, right_dim=0):
    return lax.dot_general(
        left, right, (((left_dim,), (right_dim,)), ((), ())), preferred_element_type=jnp.float32
    )


def split_dot(left, right):
    high = right.astype(jnp.bfloat16)
    low = (right - high.astype(jnp.float32)).astype(jnp.bfloat16)
    return dot(left, high) + dot(left, low)


def pack_kernel(own_ref, ids_ref, states_ref, out_ref):
    out_ref[...] = states_ref[...].astype(jnp.bfloat16)


def pack(own, send_ids, states):
    _, heads, rows, cols = states.shape
    count = send_ids.shape[0]
    block = (1, heads, rows, cols)
    return pl.pallas_call(
        pack_kernel,
        out_shape=jax.ShapeDtypeStruct((count, heads, rows, cols), jnp.bfloat16),
        grid_spec=pltpu.PrefetchScalarGridSpec(
            num_scalar_prefetch=2,
            grid=(count,),
            in_specs=[pl.BlockSpec(block, lambda j, own, ids: (ids[j, own[0]], 0, 0, 0))],
            out_specs=pl.BlockSpec(block, lambda j, own, ids: (j, 0, 0, 0)),
        ),
        compiler_params=params(),
        name="pack",
    )(own, send_ids, states)


def copy_kernel(in_ref, out_ref):
    out_ref[...] = in_ref[...]


def copied(array):
    return pl.pallas_call(
        copy_kernel,
        out_shape=jax.ShapeDtypeStruct(array.shape, array.dtype),
        compiler_params=params(0),
        name="copied",
    )(array)


def head_norm(inputs):
    return inputs * lax.rsqrt(jnp.mean(inputs * inputs, axis=-1, keepdims=True) + EPS)


def fade_row(exponent):
    return jnp.exp(jnp.full((1, DK), exponent))


def decode_rows(ref):
    return jnp.concatenate([ref[step].astype(jnp.float32) for step in range(ref.shape[0])], axis=0)


def own_kernel(
    place_ref, partner_ref, ids_ref, count_ref, slot_ref, len_ref, decode_ref, slopes_ref,
    states_ref, q_ref, k_ref, v_ref, qd_ref, kd_ref, vd_ref, mine_ref, theirs_ref,
    att_ref, dec_ref, mine_out_ref, theirs_out_ref, mem_ref,
):
    mine_out_ref[0] = mine_ref[...]
    theirs_out_ref[0] = theirs_ref[...]
    slope = slopes_ref[pl.program_id(0)]
    own = place_ref[0]
    mate = partner_ref[own]
    length = len_ref[0]
    prefill_slot = slot_ref[0]

    def kept(slot):
        gone = jnp.bool_(False)
        for entry in range(ids_ref.shape[0]):
            gone |= (ids_ref[entry, own] == slot) & (entry < count_ref[own])
            gone |= (ids_ref[entry, mate] == slot) & (entry < count_ref[mate])
        return jnp.where(gone, 0.0, states_ref[slot, 0])

    rows = lax.broadcasted_iota(jnp.int32, (BLK, BLK), 0)
    cols = lax.broadcasted_iota(jnp.int32, (BLK, BLK), 1)
    damping = jnp.exp(-slope * jnp.maximum(rows - cols, 0).astype(jnp.float32))
    leading = jnp.exp(-slope * (rows + 1).astype(jnp.float32))
    mem_ref[...] = kept(prefill_slot)

    def step(block, carry):
        count = jnp.clip(length - block * BLK, 0, BLK)
        here = pl.ds(pl.multiple_of(block * BLK, BLK), BLK)
        q_block, k_block, v_block = q_ref[here, :], k_ref[here, :], v_ref[here, :]
        memory = mem_ref[...]
        scores = dot(q_block, k_block, 1, 1)
        valid = (cols <= rows) & (cols < count)
        probs = jnp.where(valid, scores * damping, 0.0).astype(jnp.bfloat16)
        att_ref[here, :] = dot(probs, v_block) + leading * split_dot(q_block, memory)
        behind = jnp.maximum(count - 1 - rows, 0).astype(jnp.float32)
        trailing = jnp.where(rows < count, jnp.exp(-slope * behind), 0.0)
        weighted = (k_block.astype(jnp.float32) * trailing).astype(jnp.bfloat16)
        mem_ref[...] = fade_row(-slope * count.astype(jnp.float32)) * memory + dot(
            weighted, v_block, 0, 0
        )
        return carry

    lax.fori_loop(0, q_ref.shape[0] // BLK, step, 0)

    keep = fade_row(-slope)
    slots = decode_ref.shape[1]
    queries, keys, values = (decode_rows(ref) for ref in (qd_ref, kd_ref, vd_ref))
    padded = jnp.concatenate([queries, queries], axis=0).astype(jnp.bfloat16)
    place = lax.broadcasted_iota(jnp.int32, (2 * slots, DK), 0)
    seen = jnp.zeros((2 * slots, DK), jnp.float32)
    for row in range(slots):
        slot = decode_ref[0, row]
        memory = jnp.where(slot == prefill_slot, mem_ref[...], kept(slot))
        seen = jnp.where(place % slots == row, split_dot(padded, memory)[: 2 * slots], seen)
    product = lambda q, k: jnp.sum(q * k, axis=-1, keepdims=True)
    first, second = slice(0, slots), slice(slots, 2 * slots)
    now = product(queries, keys) * values
    before = product(queries[second], keys[first]) * values[first]
    dec_ref[first, :] = keep * seen[first] + now[first]
    dec_ref[second, :] = keep * (keep * seen[second] + before) + now[second]


def far_chip(place, step):
    away = jnp.where(
        step == 0, ORDER[0], jnp.where(step == 1, ORDER[1], jnp.where(step == 2, ORDER[2], ORDER[3]))
    )
    return lax.rem(place[1] // 2 + away, 4)


def own_part(place, scalars, states, prefill, decode, w_out):
    slots, heads = states.shape[:2]
    tokens, width = prefill[0].shape
    cols = w_out.shape[1] // 8
    steps = decode[0].shape[0]
    column = pl.BlockSpec((tokens, DK), lambda h, *_: (0, h))
    row = pl.BlockSpec((steps, slots, DK), lambda h, *_: (0, 0, h))
    taken = pl.BlockSpec((1, width, cols), lambda h, *_: (h, 0, 0))

    def weights(other):
        def index(h, place, *_):
            core = lax.rem(place[1], 2)
            return (0, 2 * far_chip(place, h) + (1 - core if other else core))

        return pl.BlockSpec((width, cols), index)

    return pl.pallas_call(
        own_kernel,
        out_shape=(
            jax.ShapeDtypeStruct((tokens, width), jnp.float32),
            jax.ShapeDtypeStruct((steps * slots, width), jnp.float32),
            jax.ShapeDtypeStruct((4, width, cols), jnp.bfloat16),
            jax.ShapeDtypeStruct((4, width, cols), jnp.bfloat16),
        ),
        grid_spec=pltpu.PrefetchScalarGridSpec(
            num_scalar_prefetch=8,
            grid=(heads,),
            in_specs=[
                pl.BlockSpec((slots, 1, DK, DK), lambda h, *_: (0, h, 0, 0)),
                column,
                column,
                column,
                row,
                row,
                row,
                weights(False),
                weights(True),
            ],
            out_specs=(
                column,
                pl.BlockSpec((steps * slots, DK), lambda h, *_: (0, h)),
                taken,
                taken,
            ),
            scratch_shapes=[pltpu.VMEM((DK, DK), jnp.float32)],
        ),
        compiler_params=params(),
        cost_estimate=pl.CostEstimate(
            flops=10 * tokens * BLK * width,
            bytes_accessed=5 * tokens * width * 2 + 4 * w_out.size,
            transcendentals=0,
        ),
        name="own_part",
    )(place, *scalars, states, *prefill, *decode, w_out, w_out)


def serve_kernel(
    place_ref, partner_ref, ids_ref, count_ref, slot_ref, len_ref, decode_ref, slopes_ref,
    payload_ref, att_ref, dec_ref, q_ref, qd_ref, theirs_ref, normed_ref, first_ref,
):
    first_ref[...] = theirs_ref[...]
    tokens, width = q_ref.shape
    mate = partner_ref[place_ref[0]]
    prefill_slot = slot_ref[0]
    length = len_ref[0]
    slots = decode_ref.shape[1]
    entries = ids_ref.shape[0]
    lands = [
        lambda slot, e=e: ((ids_ref[e, mate] == slot) & (e < count_ref[mate])) for e in range(entries)
    ]
    rows = lax.broadcasted_iota(jnp.int32, (tokens, DK), 0)
    place = lax.broadcasted_iota(jnp.int32, (2 * slots, DK), 0)
    later = (rows + 1).astype(jnp.float32)
    is_valid = rows < length
    for head in range(width // DK):
        here = slice(head * DK, (head + 1) * DK)
        slope = slopes_ref[head]
        chosen = jnp.zeros((DK, DK), jnp.bfloat16)
        for entry in range(entries):
            chosen = jnp.where(lands[entry](prefill_slot), payload_ref[entry, head], chosen)
        attended = att_ref[:, here] + jnp.exp(-slope * later) * dot(q_ref[:, here], chosen)
        normed = jnp.where(is_valid, head_norm(attended), 0.0)
        normed_ref[:tokens, here] = normed.astype(jnp.bfloat16)

        keep = fade_row(-slope)
        faded = fade_row(-slope * length.astype(jnp.float32))
        queries = decode_rows(qd_ref.at[:, :, here])
        padded = jnp.concatenate([queries, queries], axis=0).astype(jnp.bfloat16)
        scale = jnp.where(place < slots, keep, keep * keep)
        decoded = dec_ref[:, here]
        for entry in range(entries):
            seen = dot(padded, payload_ref[entry, head])[: 2 * slots]
            share = jnp.zeros((2 * slots, DK), jnp.float32)
            for row in range(slots):
                slot = decode_ref[0, row]
                factor = jnp.where(slot == prefill_slot, faded, 1.0)
                factor = jnp.where(lands[entry](slot), factor, 0.0)
                share = jnp.where(place % slots == row, factor, share)
            decoded += scale * share * seen
        decoded = head_norm(decoded)
        padding = jnp.zeros((PAD - 2 * slots, DK), jnp.float32)
        decoded = jnp.concatenate([decoded, padding], axis=0)
        normed_ref[tokens:, here] = decoded.astype(jnp.bfloat16)


def serve(place, scalars, payload, attended, decoded, q_prefill, q_decode, theirs):
    tokens, width = q_prefill.shape
    scalar = pl.BlockSpec(memory_space=pltpu.SMEM)
    whole = pl.BlockSpec(memory_space=pltpu.VMEM)
    first = pl.BlockSpec((1, *theirs.shape[1:]), lambda i: (0, 0, 0))
    return pl.pallas_call(
        serve_kernel,
        out_shape=(
            jax.ShapeDtypeStruct((tokens + PAD, width), jnp.bfloat16),
            jax.ShapeDtypeStruct((1, *theirs.shape[1:]), theirs.dtype),
        ),
        grid=(1,),
        in_specs=[scalar] * 8 + [whole] * 5 + [first],
        out_specs=(whole, first),
        compiler_params=params(),
        name="serve",
    )(place, *scalars, payload, attended, decoded, q_prefill, q_decode, theirs)


def join_kernel(own_ref, other_ref, *refs):
    count = len(refs) // 3
    for mine_ref, theirs_ref, out_ref in zip(refs[:count], refs[count : 2 * count], refs[2 * count :]):
        total = dot(own_ref[...], mine_ref[0]) + dot(other_ref[...], theirs_ref[0])
        out_ref[...] = total.astype(jnp.bfloat16)


def join(own, other, mine, theirs, chips):
    whole = pl.BlockSpec(memory_space=pltpu.VMEM)
    count = len(chips)
    shape = (own.shape[0], mine.shape[2])
    blocks = [pl.BlockSpec((1, *mine.shape[1:]), lambda i, chip=chip: (chip, 0, 0)) for chip in chips]
    return pl.pallas_call(
        join_kernel,
        out_shape=(jax.ShapeDtypeStruct(shape, jnp.bfloat16),) * count,
        grid=(1,),
        in_specs=[whole] * 2 + blocks * 2,
        out_specs=(whole,) * count,
        compiler_params=params(),
        name=f"join{chips[0]}",
        cost_estimate=pl.CostEstimate(
            flops=4 * count * own.size * mine.shape[2],
            bytes_accessed=4 * own.size + 4 * count * mine.shape[1] * mine.shape[2],
            transcendentals=0,
        ),
    )(own, other, *[mine] * count, *[theirs] * count)


def add_kernel(a_ref, b_ref, out_ref):
    out_ref[...] = a_ref[...].astype(jnp.float32) + b_ref[...].astype(jnp.float32)


def add(a, b):
    return pl.pallas_call(
        add_kernel,
        out_shape=jax.ShapeDtypeStruct(a.shape, jnp.float32),
        compiler_params=params(0),
        name="add",
    )(a, b)


def finish_kernel(a_ref, b_ref, c_ref, prefill_ref, decode_ref):
    total = a_ref[...] + b_ref[...].astype(jnp.float32) + c_ref[...].astype(jnp.float32)
    tokens = prefill_ref.shape[0]
    prefill_ref[...] = total[:tokens].astype(jnp.bfloat16)
    steps, slots, _ = decode_ref.shape
    for step in range(steps):
        first = tokens + step * slots
        decode_ref[step] = total[first : first + slots].astype(jnp.bfloat16)


def finish(total, near, tokens, steps, slots):
    cols = total.shape[1]
    return pl.pallas_call(
        finish_kernel,
        out_shape=(
            jax.ShapeDtypeStruct((tokens, cols), jnp.bfloat16),
            jax.ShapeDtypeStruct((steps, slots, cols), jnp.bfloat16),
        ),
        compiler_params=params(0),
        name="finish",
    )(total, *near)


def siblings():
    return [(i, i ^ 1) for i in range(lax.axis_size("head"))]


def swapped(partner, array):
    return lax.cond(
        partner[0] >= 0, lambda own: lax.ppermute(own, "head", siblings()), jnp.zeros_like, array
    )


def exchange(array, pattern):
    size = lax.axis_size("replica")
    return lax.ppermute(array, "replica", [(i, i ^ pattern) for i in range(size)])


def on_device(
    states,
    partner,
    send_ids,
    send_count,
    prefill_slot,
    prompt_len,
    decode_slots,
    q_prefill,
    k_prefill,
    v_prefill,
    q_decode,
    k_decode,
    v_decode,
    slopes,
    w_out,
):
    size = lax.axis_size("replica")
    own = lax.axis_index("replica")
    head = lax.axis_index("head")
    place = jnp.stack([own, head]).astype(jnp.int32)
    ids = send_ids.T
    scalars = (partner, ids, send_count, prefill_slot, prompt_len, decode_slots, slopes)
    devices = lax.axis_size("head")

    pattern = jnp.clip(partner[0], 1, size - 1)
    half, across = size // 2, size // 4 * 3

    def hop(*arrays):
        return exchange(pack(*arrays), across)

    payload = lax.cond(pattern >= half, hop, pack, place, ids, states)

    def branch(rest, payload, *arrays):
        moving = exchange(payload, rest) if rest else copied(payload)
        attended, decoded, mine, theirs = own_part(*arrays)
        return moving, attended, decoded, mine, swapped(partner, theirs)

    payload, attended, decoded, mine, theirs = lax.switch(
        jnp.where(pattern >= half, pattern ^ across, pattern),
        [partial(branch, rest) for rest in range(half)],
        payload,
        place,
        scalars,
        states,
        (q_prefill, k_prefill, v_prefill),
        (q_decode, k_decode, v_decode),
        w_out,
    )
    normed, first = serve(
        place, scalars, payload, attended, decoded, q_prefill, q_decode, theirs
    )
    other = lax.ppermute(normed, "head", siblings())

    def along(part, away):
        return lax.ppermute(part, "head", [(i, (i + 2 * away) % devices) for i in range(devices)])

    (farthest,) = join(normed, other, mine, first, (0,))
    farthest, normed = lax.optimization_barrier((farthest, normed))
    *near, here = join(normed, other, mine, theirs, (1, 2, 3))
    near = [along(part, away) for part, away in zip(near, ORDER[1:-1], strict=True)]
    total = add(along(farthest, ORDER[0]), here)
    steps, slots = q_decode.shape[:2]
    return finish(total, near, q_prefill.shape[0], steps, slots)


def solution(mesh):
    return jax.shard_map(
        on_device,
        mesh=mesh,
        in_specs=(
            P("replica", "head", None, None),
            P(),
            P(),
            P(),
            P("replica"),
            P("replica"),
            P("replica", None),
            P("replica", "head"),
            P("replica", "head"),
            P("replica", "head"),
            P(None, "replica", "head"),
            P(None, "replica", "head"),
            P(None, "replica", "head"),
            P("head"),
            P("head", None),
        ),
        out_specs=(P("replica", "head"), P(None, "replica", "head")),
        check_vma=False,
    )
```

```python
from functools import partial

import jax
import jax.numpy as jnp
from jax import lax
from jax.experimental import pallas as pl
from jax.experimental.pallas import tpu as pltpu
from jax.sharding import PartitionSpec as P

DK = 128
BLK = 128
EPS = 1e-06
PAD = 16
VMEM_LIMIT = 48 * 1024 * 1024
ORDER = (2, 1, 3, 0)


def params(axes=1):
    return pltpu.CompilerParams(
        dimension_semantics=("arbitrary",) * axes, vmem_limit_bytes=VMEM_LIMIT
    )


def dot(left, right, left_dim=1, right_dim=0):
    return lax.dot_general(
        left, right, (((left_dim,), (right_dim,)), ((), ())), preferred_element_type=jnp.float32
    )


def split_dot(left, right):
    high = right.astype(jnp.bfloat16)
    low = (right - high.astype(jnp.float32)).astype(jnp.bfloat16)
    return dot(left, high) + dot(left, low)


def pack_kernel(own_ref, ids_ref, states_ref, out_ref):
    out_ref[...] = states_ref[...].astype(jnp.bfloat16)


def pack(own, send_ids, states):
    _, heads, rows, cols = states.shape
    count = send_ids.shape[0]
    block = (1, heads, rows, cols)
    return pl.pallas_call(
        pack_kernel,
        out_shape=jax.ShapeDtypeStruct((count, heads, rows, cols), jnp.bfloat16),
        grid_spec=pltpu.PrefetchScalarGridSpec(
            num_scalar_prefetch=2,
            grid=(count,),
            in_specs=[pl.BlockSpec(block, lambda j, own, ids: (ids[j, own[0]], 0, 0, 0))],
            out_specs=pl.BlockSpec(block, lambda j, own, ids: (j, 0, 0, 0)),
        ),
        compiler_params=params(),
        name="pack",
    )(own, send_ids, states)


def copy_kernel(in_ref, out_ref):
    out_ref[...] = in_ref[...]


def copied(array):
    return pl.pallas_call(
        copy_kernel,
        out_shape=jax.ShapeDtypeStruct(array.shape, array.dtype),
        compiler_params=params(0),
        name="copied",
    )(array)


def head_norm(inputs):
    return inputs * lax.rsqrt(jnp.mean(inputs * inputs, axis=-1, keepdims=True) + EPS)


def fade_row(exponent):
    return jnp.exp(jnp.full((1, DK), exponent))


def decode_rows(ref):
    return jnp.concatenate([ref[step].astype(jnp.float32) for step in range(ref.shape[0])], axis=0)


def own_kernel(
    place_ref, partner_ref, ids_ref, count_ref, slot_ref, len_ref, decode_ref, slopes_ref,
    states_ref, q_ref, k_ref, v_ref, qd_ref, kd_ref, vd_ref,
    w_ref, att_ref, dec_ref, mine_out_ref, theirs_out_ref, info_ref, mem_ref, sems,
):
    info_ref[0] = slot_ref[0]
    info_ref[1] = len_ref[0]
    width, cols = mine_out_ref.shape[1:]
    chip, core = far_chip(place_ref, pl.program_id(0)), lax.rem(place_ref[1], 2)
    taken = [
        pltpu.make_async_copy(
            w_ref.at[:, pl.ds(pl.multiple_of((2 * chip + of) * cols, cols), cols)], out.at[0], sem
        )
        for of, out, sem in (
            (core, mine_out_ref, sems.at[0]),
            (1 - core, theirs_out_ref, sems.at[1]),
        )
    ]
    for copy in taken:
        copy.start()
    slope = slopes_ref[pl.program_id(0)]
    own = place_ref[0]
    mate = partner_ref[own]
    length = len_ref[0]
    prefill_slot = slot_ref[0]

    def kept(slot):
        gone = jnp.bool_(False)
        for entry in range(ids_ref.shape[0]):
            gone |= (ids_ref[entry, own] == slot) & (entry < count_ref[own])
            gone |= (ids_ref[entry, mate] == slot) & (entry < count_ref[mate])
        return jnp.where(gone, 0.0, states_ref[slot, 0])

    rows = lax.broadcasted_iota(jnp.int32, (BLK, BLK), 0)
    cols = lax.broadcasted_iota(jnp.int32, (BLK, BLK), 1)
    damping = jnp.exp(-slope * jnp.maximum(rows - cols, 0).astype(jnp.float32))
    leading = jnp.exp(-slope * (rows + 1).astype(jnp.float32))
    mem_ref[...] = kept(prefill_slot)

    def step(block, carry):
        count = jnp.clip(length - block * BLK, 0, BLK)
        here = pl.ds(pl.multiple_of(block * BLK, BLK), BLK)
        q_block, k_block, v_block = q_ref[here, :], k_ref[here, :], v_ref[here, :]
        memory = mem_ref[...]
        scores = dot(q_block, k_block, 1, 1)
        valid = (cols <= rows) & (cols < count)
        probs = jnp.where(valid, scores * damping, 0.0).astype(jnp.bfloat16)
        att_ref[here, :] = dot(probs, v_block) + leading * split_dot(q_block, memory)
        behind = jnp.maximum(count - 1 - rows, 0).astype(jnp.float32)
        trailing = jnp.where(rows < count, jnp.exp(-slope * behind), 0.0)
        weighted = (k_block.astype(jnp.float32) * trailing).astype(jnp.bfloat16)
        mem_ref[...] = fade_row(-slope * count.astype(jnp.float32)) * memory + dot(
            weighted, v_block, 0, 0
        )
        return carry

    lax.fori_loop(0, q_ref.shape[0] // BLK, step, 0)

    keep = fade_row(-slope)
    slots = decode_ref.shape[1]
    queries, keys, values = (decode_rows(ref) for ref in (qd_ref, kd_ref, vd_ref))
    padded = jnp.concatenate([queries, queries], axis=0).astype(jnp.bfloat16)
    place = lax.broadcasted_iota(jnp.int32, (2 * slots, DK), 0)
    seen = jnp.zeros((2 * slots, DK), jnp.float32)
    for row in range(slots):
        slot = decode_ref[0, row]
        memory = jnp.where(slot == prefill_slot, mem_ref[...], kept(slot))
        seen = jnp.where(place % slots == row, split_dot(padded, memory)[: 2 * slots], seen)
    product = lambda q, k: jnp.sum(q * k, axis=-1, keepdims=True)
    first, second = slice(0, slots), slice(slots, 2 * slots)
    now = product(queries, keys) * values
    before = product(queries[second], keys[first]) * values[first]
    dec_ref[first, :] = keep * seen[first] + now[first]
    dec_ref[second, :] = keep * (keep * seen[second] + before) + now[second]
    for copy in taken:
        copy.wait()


def far_chip(place, step):
    away = jnp.where(
        step == 0, ORDER[0], jnp.where(step == 1, ORDER[1], jnp.where(step == 2, ORDER[2], ORDER[3]))
    )
    return lax.rem(place[1] // 2 + away, 4)


def own_part(place, scalars, states, prefill, decode, w_out):
    slots, heads = states.shape[:2]
    tokens, width = prefill[0].shape
    cols = w_out.shape[1] // 8
    steps = decode[0].shape[0]
    column = pl.BlockSpec((tokens, DK), lambda h, *_: (0, h))
    row = pl.BlockSpec((steps, slots, DK), lambda h, *_: (0, 0, h))
    taken = pl.BlockSpec((1, width, cols), lambda h, *_: (h, 0, 0))

    return pl.pallas_call(
        own_kernel,
        out_shape=(
            jax.ShapeDtypeStruct((tokens, width), jnp.float32),
            jax.ShapeDtypeStruct((steps * slots, width), jnp.float32),
            jax.ShapeDtypeStruct((4, width, cols), jnp.bfloat16),
            jax.ShapeDtypeStruct((4, width, cols), jnp.bfloat16),
            jax.ShapeDtypeStruct((2,), jnp.int32),
        ),
        grid_spec=pltpu.PrefetchScalarGridSpec(
            num_scalar_prefetch=8,
            grid=(heads,),
            in_specs=[
                pl.BlockSpec((slots, 1, DK, DK), lambda h, *_: (0, h, 0, 0)),
                column,
                column,
                column,
                row,
                row,
                row,
                pl.BlockSpec(memory_space=pl.ANY),
            ],
            out_specs=(
                column,
                pl.BlockSpec((steps * slots, DK), lambda h, *_: (0, h)),
                taken,
                taken,
                pl.BlockSpec(memory_space=pltpu.SMEM),
            ),
            scratch_shapes=[pltpu.VMEM((DK, DK), jnp.float32), pltpu.SemaphoreType.DMA((2,))],
        ),
        compiler_params=params(),
        cost_estimate=pl.CostEstimate(
            flops=10 * tokens * BLK * width,
            bytes_accessed=5 * tokens * width * 2 + 4 * w_out.size,
            transcendentals=0,
        ),
        name="own_part",
    )(place, *scalars, states, *prefill, *decode, w_out)


def serve_kernel(
    place_ref, partner_ref, ids_ref, count_ref, info_ref, decode_ref, slopes_ref,
    payload_ref, att_ref, dec_ref, q_ref, qd_ref, theirs_ref, normed_ref, first_ref,
):
    first_ref[...] = theirs_ref[...]
    tokens, width = q_ref.shape
    mate = partner_ref[place_ref[0]]
    prefill_slot = info_ref[0]
    length = info_ref[1]
    slots = decode_ref.shape[1]
    entries = ids_ref.shape[0]
    lands = [
        lambda slot, e=e: ((ids_ref[e, mate] == slot) & (e < count_ref[mate])) for e in range(entries)
    ]
    rows = lax.broadcasted_iota(jnp.int32, (tokens, DK), 0)
    place = lax.broadcasted_iota(jnp.int32, (2 * slots, DK), 0)
    later = (rows + 1).astype(jnp.float32)
    is_valid = rows < length
    for head in range(width // DK):
        here = slice(head * DK, (head + 1) * DK)
        slope = slopes_ref[head]
        chosen = jnp.zeros((DK, DK), jnp.bfloat16)
        for entry in range(entries):
            chosen = jnp.where(lands[entry](prefill_slot), payload_ref[entry, head], chosen)
        attended = att_ref[:, here] + jnp.exp(-slope * later) * dot(q_ref[:, here], chosen)
        normed = jnp.where(is_valid, head_norm(attended), 0.0)
        normed_ref[:tokens, here] = normed.astype(jnp.bfloat16)

        keep = fade_row(-slope)
        faded = fade_row(-slope * length.astype(jnp.float32))
        queries = decode_rows(qd_ref.at[:, :, here])
        padded = jnp.concatenate([queries, queries], axis=0).astype(jnp.bfloat16)
        scale = jnp.where(place < slots, keep, keep * keep)
        decoded = dec_ref[:, here]
        for entry in range(entries):
            seen = dot(padded, payload_ref[entry, head])[: 2 * slots]
            share = jnp.zeros((2 * slots, DK), jnp.float32)
            for row in range(slots):
                slot = decode_ref[0, row]
                factor = jnp.where(slot == prefill_slot, faded, 1.0)
                factor = jnp.where(lands[entry](slot), factor, 0.0)
                share = jnp.where(place % slots == row, factor, share)
            decoded += scale * share * seen
        decoded = head_norm(decoded)
        padding = jnp.zeros((PAD - 2 * slots, DK), jnp.float32)
        decoded = jnp.concatenate([decoded, padding], axis=0)
        normed_ref[tokens:, here] = decoded.astype(jnp.bfloat16)


def serve(place, scalars, payload, attended, decoded, q_prefill, q_decode, theirs):
    tokens, width = q_prefill.shape
    scalar = pl.BlockSpec(memory_space=pltpu.SMEM)
    whole = pl.BlockSpec(memory_space=pltpu.VMEM)
    first = pl.BlockSpec((1, *theirs.shape[1:]), lambda i: (0, 0, 0))
    return pl.pallas_call(
        serve_kernel,
        out_shape=(
            jax.ShapeDtypeStruct((tokens + PAD, width), jnp.bfloat16),
            jax.ShapeDtypeStruct((1, *theirs.shape[1:]), theirs.dtype),
        ),
        grid=(1,),
        in_specs=[scalar] * 7 + [whole] * 5 + [first],
        out_specs=(whole, first),
        compiler_params=params(),
        name="serve",
    )(place, *scalars, payload, attended, decoded, q_prefill, q_decode, theirs)


def join_kernel(own_ref, other_ref, *refs):
    count = len(refs) // 3
    for mine_ref, theirs_ref, out_ref in zip(refs[:count], refs[count : 2 * count], refs[2 * count :]):
        total = dot(own_ref[...], mine_ref[0]) + dot(other_ref[...], theirs_ref[0])
        out_ref[...] = total.astype(jnp.bfloat16)


def join(own, other, mine, theirs, chips):
    whole = pl.BlockSpec(memory_space=pltpu.VMEM)
    count = len(chips)
    shape = (own.shape[0], mine.shape[2])
    blocks = [pl.BlockSpec((1, *mine.shape[1:]), lambda i, chip=chip: (chip, 0, 0)) for chip in chips]
    return pl.pallas_call(
        join_kernel,
        out_shape=(jax.ShapeDtypeStruct(shape, jnp.bfloat16),) * count,
        grid=(1,),
        in_specs=[whole] * 2 + blocks * 2,
        out_specs=(whole,) * count,
        compiler_params=params(),
        name=f"join{chips[0]}",
        cost_estimate=pl.CostEstimate(
            flops=4 * count * own.size * mine.shape[2],
            bytes_accessed=4 * own.size + 4 * count * mine.shape[1] * mine.shape[2],
            transcendentals=0,
        ),
    )(own, other, *[mine] * count, *[theirs] * count)


def add_kernel(a_ref, b_ref, out_ref):
    out_ref[...] = a_ref[...].astype(jnp.float32) + b_ref[...].astype(jnp.float32)


def add(a, b):
    return pl.pallas_call(
        add_kernel,
        out_shape=jax.ShapeDtypeStruct(a.shape, jnp.float32),
        compiler_params=params(0),
        name="add",
    )(a, b)


def finish_kernel(a_ref, b_ref, c_ref, prefill_ref, decode_ref):
    total = a_ref[...] + b_ref[...].astype(jnp.float32) + c_ref[...].astype(jnp.float32)
    tokens = prefill_ref.shape[0]
    prefill_ref[...] = total[:tokens].astype(jnp.bfloat16)
    steps, slots, _ = decode_ref.shape
    for step in range(steps):
        first = tokens + step * slots
        decode_ref[step] = total[first : first + slots].astype(jnp.bfloat16)


def finish(total, near, tokens, steps, slots):
    cols = total.shape[1]
    return pl.pallas_call(
        finish_kernel,
        out_shape=(
            jax.ShapeDtypeStruct((tokens, cols), jnp.bfloat16),
            jax.ShapeDtypeStruct((steps, slots, cols), jnp.bfloat16),
        ),
        compiler_params=params(0),
        name="finish",
    )(total, *near)


def siblings():
    return [(i, i ^ 1) for i in range(lax.axis_size("head"))]


def swapped(partner, array):
    return lax.cond(
        partner[0] >= 0, lambda own: lax.ppermute(own, "head", siblings()), jnp.zeros_like, array
    )


def exchange(array, pattern):
    size = lax.axis_size("replica")
    return lax.ppermute(array, "replica", [(i, i ^ pattern) for i in range(size)])


def on_device(
    states,
    partner,
    send_ids,
    send_count,
    prefill_slot,
    prompt_len,
    decode_slots,
    q_prefill,
    k_prefill,
    v_prefill,
    q_decode,
    k_decode,
    v_decode,
    slopes,
    w_out,
):
    size = lax.axis_size("replica")
    own = lax.axis_index("replica")
    head = lax.axis_index("head")
    place = jnp.stack([own, head]).astype(jnp.int32)
    ids = send_ids.T
    scalars = (partner, ids, send_count, prefill_slot, prompt_len, decode_slots, slopes)
    devices = lax.axis_size("head")

    pattern = jnp.clip(partner[0], 1, size - 1)
    half, across = size // 2, size // 4 * 3

    def hop(*arrays):
        return exchange(pack(*arrays), across)

    payload = lax.cond(pattern >= half, hop, pack, place, ids, states)

    def branch(rest, payload, *arrays):
        moving = exchange(payload, rest) if rest else copied(payload)
        attended, decoded, mine, theirs, info = own_part(*arrays)
        return moving, attended, decoded, mine, swapped(partner, theirs), info

    payload, attended, decoded, mine, theirs, info = lax.switch(
        jnp.where(pattern >= half, pattern ^ across, pattern),
        [partial(branch, rest) for rest in range(half)],
        payload,
        place,
        scalars,
        states,
        (q_prefill, k_prefill, v_prefill),
        (q_decode, k_decode, v_decode),
        w_out,
    )
    scalars = (partner, ids, send_count, info, decode_slots, slopes)
    normed, first = serve(
        place, scalars, payload, attended, decoded, q_prefill, q_decode, theirs
    )
    other = lax.ppermute(normed, "head", siblings())

    def along(part, away):
        return lax.ppermute(part, "head", [(i, (i + 2 * away) % devices) for i in range(devices)])

    (farthest,) = join(normed, other, mine, first, (0,))
    farthest, normed = lax.optimization_barrier((farthest, normed))
    *near, here = join(normed, other, mine, theirs, (1, 2, 3))
    near = [along(part, away) for part, away in zip(near, ORDER[1:-1], strict=True)]
    total = add(along(farthest, ORDER[0]), here)
    steps, slots = q_decode.shape[:2]
    return finish(total, near, q_prefill.shape[0], steps, slots)


def solution(mesh):
    return jax.shard_map(
        on_device,
        mesh=mesh,
        in_specs=(
            P("replica", "head", None, None),
            P(),
            P(),
            P(),
            P("replica"),
            P("replica"),
            P("replica", None),
            P("replica", "head"),
            P("replica", "head"),
            P("replica", "head"),
            P(None, "replica", "head"),
            P(None, "replica", "head"),
            P(None, "replica", "head"),
            P("head"),
            P("head", None),
        ),
        out_specs=(P("replica", "head"), P(None, "replica", "head")),
        check_vma=False,
    )
```

```python
from functools import partial

import jax
import jax.numpy as jnp
from jax import lax
from jax.experimental import pallas as pl
from jax.experimental.pallas import tpu as pltpu
from jax.sharding import PartitionSpec as P

DK = 128
BLK = 128
EPS = 1e-06
PAD = 16
VMEM_LIMIT = 48 * 1024 * 1024
ORDER = (2, 1, 3, 0)


def params(axes=1):
    return pltpu.CompilerParams(
        dimension_semantics=("arbitrary",) * axes, vmem_limit_bytes=VMEM_LIMIT
    )


def dot(left, right, left_dim=1, right_dim=0):
    return lax.dot_general(
        left, right, (((left_dim,), (right_dim,)), ((), ())), preferred_element_type=jnp.float32
    )


def split_dot(left, right):
    high = right.astype(jnp.bfloat16)
    low = (right - high.astype(jnp.float32)).astype(jnp.bfloat16)
    return dot(left, high) + dot(left, low)


def pack_kernel(own_ref, ids_ref, states_ref, out_ref):
    out_ref[...] = states_ref[...].astype(jnp.bfloat16)


def pack(own, send_ids, states):
    _, heads, rows, cols = states.shape
    count = send_ids.shape[0]
    block = (1, heads, rows, cols)
    return pl.pallas_call(
        pack_kernel,
        out_shape=jax.ShapeDtypeStruct((count, heads, rows, cols), jnp.bfloat16),
        grid_spec=pltpu.PrefetchScalarGridSpec(
            num_scalar_prefetch=2,
            grid=(count,),
            in_specs=[pl.BlockSpec(block, lambda j, own, ids: (ids[j, own[0]], 0, 0, 0))],
            out_specs=pl.BlockSpec(block, lambda j, own, ids: (j, 0, 0, 0)),
        ),
        compiler_params=params(),
        name="pack",
    )(own, send_ids, states)


def copy_kernel(in_ref, out_ref):
    out_ref[...] = in_ref[...]


def copied(array):
    return pl.pallas_call(
        copy_kernel,
        out_shape=jax.ShapeDtypeStruct(array.shape, array.dtype),
        compiler_params=params(0),
        name="copied",
    )(array)


def head_norm(inputs):
    return inputs * lax.rsqrt(jnp.mean(inputs * inputs, axis=-1, keepdims=True) + EPS)


def fade_row(exponent):
    return jnp.exp(jnp.full((1, DK), exponent))


def decode_rows(ref):
    return jnp.concatenate([ref[step].astype(jnp.float32) for step in range(ref.shape[0])], axis=0)


def own_kernel(
    place_ref, partner_ref, ids_ref, count_ref, slot_ref, len_ref, decode_ref, slopes_ref,
    states_ref, q_ref, k_ref, v_ref, qd_ref, kd_ref, vd_ref,
    w_ref, att_ref, dec_ref, mine_out_ref, theirs_out_ref, info_ref, mem_ref, sems,
):
    info_ref[0] = slot_ref[0]
    info_ref[1] = len_ref[0]
    width, cols = mine_out_ref.shape[1:]
    chip, core = far_chip(place_ref, pl.program_id(0)), lax.rem(place_ref[1], 2)
    taken = [
        pltpu.make_async_copy(
            w_ref.at[:, pl.ds(pl.multiple_of((2 * chip + of) * cols, cols), cols)], out.at[0], sem
        )
        for of, out, sem in (
            (core, mine_out_ref, sems.at[0]),
            (1 - core, theirs_out_ref, sems.at[1]),
        )
    ]
    for copy in taken:
        copy.start()
    slope = slopes_ref[pl.program_id(0)]
    own = place_ref[0]
    mate = partner_ref[own]
    length = len_ref[0]
    prefill_slot = slot_ref[0]

    def kept(slot):
        gone = jnp.bool_(False)
        for entry in range(ids_ref.shape[0]):
            gone |= (ids_ref[entry, own] == slot) & (entry < count_ref[own])
            gone |= (ids_ref[entry, mate] == slot) & (entry < count_ref[mate])
        return jnp.where(gone, 0.0, states_ref[slot, 0])

    rows = lax.broadcasted_iota(jnp.int32, (BLK, BLK), 0)
    cols = lax.broadcasted_iota(jnp.int32, (BLK, BLK), 1)
    damping = jnp.exp(-slope * jnp.maximum(rows - cols, 0).astype(jnp.float32))
    leading = jnp.exp(-slope * (rows + 1).astype(jnp.float32))
    mem_ref[...] = kept(prefill_slot)

    def step(block, carry):
        count = jnp.clip(length - block * BLK, 0, BLK)
        here = pl.ds(pl.multiple_of(block * BLK, BLK), BLK)
        q_block, k_block, v_block = q_ref[here, :], k_ref[here, :], v_ref[here, :]
        memory = mem_ref[...]
        scores = dot(q_block, k_block, 1, 1)
        valid = (cols <= rows) & (cols < count)
        probs = jnp.where(valid, scores * damping, 0.0).astype(jnp.bfloat16)
        att_ref[here, :] = dot(probs, v_block) + leading * split_dot(q_block, memory)
        behind = jnp.maximum(count - 1 - rows, 0).astype(jnp.float32)
        trailing = jnp.where(rows < count, jnp.exp(-slope * behind), 0.0)
        weighted = (k_block.astype(jnp.float32) * trailing).astype(jnp.bfloat16)
        mem_ref[...] = fade_row(-slope * count.astype(jnp.float32)) * memory + dot(
            weighted, v_block, 0, 0
        )
        return carry

    lax.fori_loop(0, q_ref.shape[0] // BLK, step, 0)

    keep = fade_row(-slope)
    slots = decode_ref.shape[1]
    queries, keys, values = (decode_rows(ref) for ref in (qd_ref, kd_ref, vd_ref))
    padded = jnp.concatenate([queries, queries], axis=0).astype(jnp.bfloat16)
    place = lax.broadcasted_iota(jnp.int32, (2 * slots, DK), 0)
    seen = jnp.zeros((2 * slots, DK), jnp.float32)
    for row in range(slots):
        slot = decode_ref[0, row]
        memory = jnp.where(slot == prefill_slot, mem_ref[...], kept(slot))
        seen = jnp.where(place % slots == row, split_dot(padded, memory)[: 2 * slots], seen)
    product = lambda q, k: jnp.sum(q * k, axis=-1, keepdims=True)
    first, second = slice(0, slots), slice(slots, 2 * slots)
    now = product(queries, keys) * values
    before = product(queries[second], keys[first]) * values[first]
    dec_ref[first, :] = keep * seen[first] + now[first]
    dec_ref[second, :] = keep * (keep * seen[second] + before) + now[second]
    for copy in taken:
        copy.wait()


def far_chip(place, step):
    away = jnp.where(
        step == 0, ORDER[0], jnp.where(step == 1, ORDER[1], jnp.where(step == 2, ORDER[2], ORDER[3]))
    )
    return lax.rem(place[1] // 2 + away, 4)


def own_part(place, scalars, states, prefill, decode, w_out):
    slots, heads = states.shape[:2]
    tokens, width = prefill[0].shape
    cols = w_out.shape[1] // 8
    steps = decode[0].shape[0]
    column = pl.BlockSpec((tokens, DK), lambda h, *_: (0, h))
    row = pl.BlockSpec((steps, slots, DK), lambda h, *_: (0, 0, h))
    taken = pl.BlockSpec((1, width, cols), lambda h, *_: (h, 0, 0))

    return pl.pallas_call(
        own_kernel,
        out_shape=(
            jax.ShapeDtypeStruct((tokens, width), jnp.float32),
            jax.ShapeDtypeStruct((steps * slots, width), jnp.float32),
            jax.ShapeDtypeStruct((4, width, cols), jnp.bfloat16),
            jax.ShapeDtypeStruct((4, width, cols), jnp.bfloat16),
            jax.ShapeDtypeStruct((2,), jnp.int32),
        ),
        grid_spec=pltpu.PrefetchScalarGridSpec(
            num_scalar_prefetch=8,
            grid=(heads,),
            in_specs=[
                pl.BlockSpec((slots, 1, DK, DK), lambda h, *_: (0, h, 0, 0)),
                column,
                column,
                column,
                row,
                row,
                row,
                pl.BlockSpec(memory_space=pl.ANY),
            ],
            out_specs=(
                column,
                pl.BlockSpec((steps * slots, DK), lambda h, *_: (0, h)),
                taken,
                taken,
                pl.BlockSpec(memory_space=pltpu.SMEM),
            ),
            scratch_shapes=[pltpu.VMEM((DK, DK), jnp.float32), pltpu.SemaphoreType.DMA((2,))],
        ),
        compiler_params=params(),
        cost_estimate=pl.CostEstimate(
            flops=10 * tokens * BLK * width,
            bytes_accessed=5 * tokens * width * 2 + 4 * w_out.size,
            transcendentals=0,
        ),
        name="own_part",
    )(place, *scalars, states, *prefill, *decode, w_out)


def serve_kernel(
    place_ref, partner_ref, ids_ref, count_ref, info_ref, decode_ref, slopes_ref,
    payload_ref, att_ref, dec_ref, q_ref, qd_ref, theirs_ref, normed_ref, first_ref,
):
    first_ref[...] = theirs_ref[...]
    tokens, width = q_ref.shape
    mate = partner_ref[place_ref[0]]
    prefill_slot = info_ref[0]
    length = info_ref[1]
    slots = decode_ref.shape[1]
    entries = ids_ref.shape[0]
    place = lax.broadcasted_iota(jnp.int32, (2 * slots, DK), 0)
    lands, shares = [], []
    is_prefill = jnp.zeros((2 * slots, DK), jnp.bool_)
    for row in range(slots):
        is_prefill |= (place % slots == row) & (decode_ref[0, row] == prefill_slot)
    for entry in range(entries):
        sent = entry < count_ref[mate]
        arriving = jnp.where(sent, ids_ref[entry, mate], -1)
        lands.append(arriving == prefill_slot)
        share = jnp.zeros((2 * slots, DK), jnp.float32)
        for row in range(slots):
            share = jnp.where((place % slots == row) & (decode_ref[0, row] == arriving), 1.0, share)
        shares.append(share)
    rows = lax.broadcasted_iota(jnp.int32, (tokens, DK), 0)
    later = (rows + 1).astype(jnp.float32)
    is_valid = rows < length
    for head in range(width // DK):
        here = slice(head * DK, (head + 1) * DK)
        slope = slopes_ref[head]
        chosen = jnp.zeros((DK, DK), jnp.bfloat16)
        for entry in range(entries):
            chosen = jnp.where(lands[entry], payload_ref[entry, head], chosen)
        attended = att_ref[:, here] + jnp.exp(-slope * later) * dot(q_ref[:, here], chosen)
        normed = jnp.where(is_valid, head_norm(attended), 0.0)
        normed_ref[:tokens, here] = normed.astype(jnp.bfloat16)

        keep = fade_row(-slope)
        faded = fade_row(-slope * length.astype(jnp.float32))
        queries = decode_rows(qd_ref.at[:, :, here])
        padded = jnp.concatenate([queries, queries], axis=0).astype(jnp.bfloat16)
        scale = jnp.where(place < slots, keep, keep * keep) * jnp.where(is_prefill, faded, 1.0)
        decoded = dec_ref[:, here]
        for entry in range(entries):
            seen = dot(padded, payload_ref[entry, head])[: 2 * slots]
            decoded += scale * shares[entry] * seen
        decoded = head_norm(decoded)
        padding = jnp.zeros((PAD - 2 * slots, DK), jnp.float32)
        decoded = jnp.concatenate([decoded, padding], axis=0)
        normed_ref[tokens:, here] = decoded.astype(jnp.bfloat16)


def serve(place, scalars, payload, attended, decoded, q_prefill, q_decode, theirs):
    tokens, width = q_prefill.shape
    scalar = pl.BlockSpec(memory_space=pltpu.SMEM)
    whole = pl.BlockSpec(memory_space=pltpu.VMEM)
    first = pl.BlockSpec((1, *theirs.shape[1:]), lambda i: (0, 0, 0))
    return pl.pallas_call(
        serve_kernel,
        out_shape=(
            jax.ShapeDtypeStruct((tokens + PAD, width), jnp.bfloat16),
            jax.ShapeDtypeStruct((1, *theirs.shape[1:]), theirs.dtype),
        ),
        grid=(1,),
        in_specs=[scalar] * 7 + [whole] * 5 + [first],
        out_specs=(whole, first),
        compiler_params=params(),
        name="serve",
    )(place, *scalars, payload, attended, decoded, q_prefill, q_decode, theirs)


def join_kernel(own_ref, other_ref, *refs):
    count = len(refs) // 3
    for mine_ref, theirs_ref, out_ref in zip(refs[:count], refs[count : 2 * count], refs[2 * count :]):
        total = dot(own_ref[...], mine_ref[0]) + dot(other_ref[...], theirs_ref[0])
        out_ref[...] = total.astype(jnp.bfloat16)


def join(own, other, mine, theirs, chips):
    whole = pl.BlockSpec(memory_space=pltpu.VMEM)
    count = len(chips)
    shape = (own.shape[0], mine.shape[2])
    blocks = [pl.BlockSpec((1, *mine.shape[1:]), lambda i, chip=chip: (chip, 0, 0)) for chip in chips]
    return pl.pallas_call(
        join_kernel,
        out_shape=(jax.ShapeDtypeStruct(shape, jnp.bfloat16),) * count,
        grid=(1,),
        in_specs=[whole] * 2 + blocks * 2,
        out_specs=(whole,) * count,
        compiler_params=params(),
        name=f"join{chips[0]}",
        cost_estimate=pl.CostEstimate(
            flops=4 * count * own.size * mine.shape[2],
            bytes_accessed=4 * own.size + 4 * count * mine.shape[1] * mine.shape[2],
            transcendentals=0,
        ),
    )(own, other, *[mine] * count, *[theirs] * count)


def add_kernel(a_ref, b_ref, out_ref):
    out_ref[...] = a_ref[...].astype(jnp.float32) + b_ref[...].astype(jnp.float32)


def add(a, b):
    return pl.pallas_call(
        add_kernel,
        out_shape=jax.ShapeDtypeStruct(a.shape, jnp.float32),
        compiler_params=params(0),
        name="add",
    )(a, b)


def finish_kernel(a_ref, b_ref, c_ref, prefill_ref, decode_ref):
    total = a_ref[...] + b_ref[...].astype(jnp.float32) + c_ref[...].astype(jnp.float32)
    tokens = prefill_ref.shape[0]
    prefill_ref[...] = total[:tokens].astype(jnp.bfloat16)
    steps, slots, _ = decode_ref.shape
    for step in range(steps):
        first = tokens + step * slots
        decode_ref[step] = total[first : first + slots].astype(jnp.bfloat16)


def finish(total, near, tokens, steps, slots):
    cols = total.shape[1]
    return pl.pallas_call(
        finish_kernel,
        out_shape=(
            jax.ShapeDtypeStruct((tokens, cols), jnp.bfloat16),
            jax.ShapeDtypeStruct((steps, slots, cols), jnp.bfloat16),
        ),
        compiler_params=params(0),
        name="finish",
    )(total, *near)


def siblings():
    return [(i, i ^ 1) for i in range(lax.axis_size("head"))]


def swapped(partner, array):
    return lax.cond(
        partner[0] >= 0, lambda own: lax.ppermute(own, "head", siblings()), jnp.zeros_like, array
    )


def exchange(array, pattern):
    size = lax.axis_size("replica")
    return lax.ppermute(array, "replica", [(i, i ^ pattern) for i in range(size)])


def on_device(
    states,
    partner,
    send_ids,
    send_count,
    prefill_slot,
    prompt_len,
    decode_slots,
    q_prefill,
    k_prefill,
    v_prefill,
    q_decode,
    k_decode,
    v_decode,
    slopes,
    w_out,
):
    size = lax.axis_size("replica")
    own = lax.axis_index("replica")
    head = lax.axis_index("head")
    place = jnp.stack([own, head]).astype(jnp.int32)
    ids = send_ids.T
    scalars = (partner, ids, send_count, prefill_slot, prompt_len, decode_slots, slopes)
    devices = lax.axis_size("head")

    pattern = jnp.clip(partner[0], 1, size - 1)
    half, across = size // 2, size // 4 * 3

    def hop(payload):
        return exchange(payload, across)

    payload = lax.cond(pattern >= half, hop, copied, pack(place, ids, states))

    def branch(rest, payload, *arrays):
        moving = exchange(payload, rest) if rest else copied(payload)
        attended, decoded, mine, theirs, info = own_part(*arrays)
        return moving, attended, decoded, mine, swapped(partner, theirs), info

    payload, attended, decoded, mine, theirs, info = lax.switch(
        jnp.where(pattern >= half, pattern ^ across, pattern),
        [partial(branch, rest) for rest in range(half)],
        payload,
        place,
        scalars,
        states,
        (q_prefill, k_prefill, v_prefill),
        (q_decode, k_decode, v_decode),
        w_out,
    )
    scalars = (partner, ids, send_count, info, decode_slots, slopes)
    normed, first = serve(
        place, scalars, payload, attended, decoded, q_prefill, q_decode, theirs
    )
    other = lax.ppermute(normed, "head", siblings())

    def along(part, away):
        return lax.ppermute(part, "head", [(i, (i + 2 * away) % devices) for i in range(devices)])

    (farthest,) = join(normed, other, mine, first, (0,))
    farthest, normed = lax.optimization_barrier((farthest, normed))
    *near, here = join(normed, other, mine, theirs, (1, 2, 3))
    near = [along(part, away) for part, away in zip(near, ORDER[1:-1], strict=True)]
    total = add(along(farthest, ORDER[0]), here)
    steps, slots = q_decode.shape[:2]
    return finish(total, near, q_prefill.shape[0], steps, slots)


def solution(mesh):
    return jax.shard_map(
        on_device,
        mesh=mesh,
        in_specs=(
            P("replica", "head", None, None),
            P(),
            P(),
            P(),
            P("replica"),
            P("replica"),
            P("replica", None),
            P("replica", "head"),
            P("replica", "head"),
            P("replica", "head"),
            P(None, "replica", "head"),
            P(None, "replica", "head"),
            P(None, "replica", "head"),
            P("head"),
            P("head", None),
        ),
        out_specs=(P("replica", "head"), P(None, "replica", "head")),
        check_vma=False,
    )
```

```python
from functools import partial

import jax
import jax.numpy as jnp
from jax import lax
from jax.experimental import pallas as pl
from jax.experimental.pallas import tpu as pltpu
from jax.sharding import PartitionSpec as P

DK = 128
BLK = 128
EPS = 1e-06
PAD = 16
VMEM_LIMIT = 48 * 1024 * 1024
ORDER = (2, 1, 3, 0)


def params(axes=1):
    return pltpu.CompilerParams(
        dimension_semantics=("arbitrary",) * axes, vmem_limit_bytes=VMEM_LIMIT
    )


def dot(left, right, left_dim=1, right_dim=0):
    return lax.dot_general(
        left, right, (((left_dim,), (right_dim,)), ((), ())), preferred_element_type=jnp.float32
    )


def split_dot(left, right):
    high = right.astype(jnp.bfloat16)
    low = (right - high.astype(jnp.float32)).astype(jnp.bfloat16)
    return dot(left, high) + dot(left, low)


def pack_kernel(own_ref, ids_ref, states_ref, out_ref):
    out_ref[...] = states_ref[...].astype(jnp.bfloat16)


def pack(own, send_ids, states):
    _, heads, rows, cols = states.shape
    count = send_ids.shape[0]
    block = (1, heads, rows, cols)
    return pl.pallas_call(
        pack_kernel,
        out_shape=jax.ShapeDtypeStruct((count, heads, rows, cols), jnp.bfloat16),
        grid_spec=pltpu.PrefetchScalarGridSpec(
            num_scalar_prefetch=2,
            grid=(count,),
            in_specs=[pl.BlockSpec(block, lambda j, own, ids: (ids[j, own[0]], 0, 0, 0))],
            out_specs=pl.BlockSpec(block, lambda j, own, ids: (j, 0, 0, 0)),
        ),
        compiler_params=params(),
        name="pack",
    )(own, send_ids, states)


def copy_kernel(in_ref, out_ref):
    out_ref[...] = in_ref[...]


def copied(array):
    return pl.pallas_call(
        copy_kernel,
        out_shape=jax.ShapeDtypeStruct(array.shape, array.dtype),
        compiler_params=params(0),
        name="copied",
    )(array)


def head_norm(inputs):
    return inputs * lax.rsqrt(jnp.mean(inputs * inputs, axis=-1, keepdims=True) + EPS)


def fade_row(exponent):
    return jnp.exp(jnp.full((1, DK), exponent))


def decode_rows(ref):
    return jnp.concatenate([ref[step].astype(jnp.float32) for step in range(ref.shape[0])], axis=0)


def own_kernel(
    place_ref, partner_ref, ids_ref, count_ref, slot_ref, len_ref, decode_ref, slopes_ref,
    states_ref, q_ref, k_ref, v_ref, qd_ref, kd_ref, vd_ref,
    w_ref, att_ref, dec_ref, mine_out_ref, theirs_out_ref, info_ref, mem_ref, sems,
):
    info_ref[0] = slot_ref[0]
    info_ref[1] = len_ref[0]
    width, cols = mine_out_ref.shape[1:]
    chip, core = far_chip(place_ref, pl.program_id(0)), lax.rem(place_ref[1], 2)
    taken = [
        pltpu.make_async_copy(
            w_ref.at[:, pl.ds(pl.multiple_of((2 * chip + of) * cols, cols), cols)], out.at[0], sem
        )
        for of, out, sem in (
            (core, mine_out_ref, sems.at[0]),
            (1 - core, theirs_out_ref, sems.at[1]),
        )
    ]
    for copy in taken:
        copy.start()
    slope = slopes_ref[pl.program_id(0)]
    own = place_ref[0]
    mate = partner_ref[own]
    length = len_ref[0]
    prefill_slot = slot_ref[0]

    def kept(slot):
        gone = jnp.bool_(False)
        for entry in range(ids_ref.shape[0]):
            gone |= (ids_ref[entry, own] == slot) & (entry < count_ref[own])
            gone |= (ids_ref[entry, mate] == slot) & (entry < count_ref[mate])
        return jnp.where(gone, 0.0, states_ref[slot, 0])

    rows = lax.broadcasted_iota(jnp.int32, (BLK, BLK), 0)
    cols = lax.broadcasted_iota(jnp.int32, (BLK, BLK), 1)
    damping = jnp.exp(-slope * jnp.maximum(rows - cols, 0).astype(jnp.float32))
    leading = jnp.exp(-slope * (rows + 1).astype(jnp.float32))
    mem_ref[...] = kept(prefill_slot)

    def step(block, carry):
        count = jnp.clip(length - block * BLK, 0, BLK)
        here = pl.ds(pl.multiple_of(block * BLK, BLK), BLK)
        q_block, k_block, v_block = q_ref[here, :], k_ref[here, :], v_ref[here, :]
        memory = mem_ref[...]
        scores = dot(q_block, k_block, 1, 1)
        valid = (cols <= rows) & (cols < count)
        probs = jnp.where(valid, scores * damping, 0.0).astype(jnp.bfloat16)
        att_ref[here, :] = dot(probs, v_block) + leading * dot(q_block, memory.astype(jnp.bfloat16))
        behind = jnp.maximum(count - 1 - rows, 0).astype(jnp.float32)
        trailing = jnp.where(rows < count, jnp.exp(-slope * behind), 0.0)
        weighted = (k_block.astype(jnp.float32) * trailing).astype(jnp.bfloat16)
        mem_ref[...] = fade_row(-slope * count.astype(jnp.float32)) * memory + dot(
            weighted, v_block, 0, 0
        )
        return carry

    lax.fori_loop(0, q_ref.shape[0] // BLK, step, 0, unroll=2)

    keep = fade_row(-slope)
    slots = decode_ref.shape[1]
    queries, keys, values = (decode_rows(ref) for ref in (qd_ref, kd_ref, vd_ref))
    padded = jnp.concatenate([queries, queries], axis=0).astype(jnp.bfloat16)
    place = lax.broadcasted_iota(jnp.int32, (2 * slots, DK), 0)
    seen = jnp.zeros((2 * slots, DK), jnp.float32)
    for row in range(slots):
        slot = decode_ref[0, row]
        memory = jnp.where(slot == prefill_slot, mem_ref[...], kept(slot))
        seen = jnp.where(place % slots == row, split_dot(padded, memory)[: 2 * slots], seen)
    product = lambda q, k: jnp.sum(q * k, axis=-1, keepdims=True)
    first, second = slice(0, slots), slice(slots, 2 * slots)
    now = product(queries, keys) * values
    before = product(queries[second], keys[first]) * values[first]
    dec_ref[first, :] = keep * seen[first] + now[first]
    dec_ref[second, :] = keep * (keep * seen[second] + before) + now[second]
    for copy in taken:
        copy.wait()


def far_chip(place, step):
    away = jnp.where(
        step == 0, ORDER[0], jnp.where(step == 1, ORDER[1], jnp.where(step == 2, ORDER[2], ORDER[3]))
    )
    return lax.rem(place[1] // 2 + away, 4)


def own_part(place, scalars, states, prefill, decode, w_out):
    slots, heads = states.shape[:2]
    tokens, width = prefill[0].shape
    cols = w_out.shape[1] // 8
    steps = decode[0].shape[0]
    column = pl.BlockSpec((tokens, DK), lambda h, *_: (0, h))
    row = pl.BlockSpec((steps, slots, DK), lambda h, *_: (0, 0, h))
    taken = pl.BlockSpec((1, width, cols), lambda h, *_: (h, 0, 0))

    return pl.pallas_call(
        own_kernel,
        out_shape=(
            jax.ShapeDtypeStruct((tokens, width), jnp.float32),
            jax.ShapeDtypeStruct((steps * slots, width), jnp.float32),
            jax.ShapeDtypeStruct((4, width, cols), jnp.bfloat16),
            jax.ShapeDtypeStruct((4, width, cols), jnp.bfloat16),
            jax.ShapeDtypeStruct((2,), jnp.int32),
        ),
        grid_spec=pltpu.PrefetchScalarGridSpec(
            num_scalar_prefetch=8,
            grid=(heads,),
            in_specs=[
                pl.BlockSpec((slots, 1, DK, DK), lambda h, *_: (0, h, 0, 0)),
                column,
                column,
                column,
                row,
                row,
                row,
                pl.BlockSpec(memory_space=pl.ANY),
            ],
            out_specs=(
                column,
                pl.BlockSpec((steps * slots, DK), lambda h, *_: (0, h)),
                taken,
                taken,
                pl.BlockSpec(memory_space=pltpu.SMEM),
            ),
            scratch_shapes=[pltpu.VMEM((DK, DK), jnp.float32), pltpu.SemaphoreType.DMA((2,))],
        ),
        compiler_params=params(),
        cost_estimate=pl.CostEstimate(
            flops=10 * tokens * BLK * width,
            bytes_accessed=5 * tokens * width * 2 + 4 * w_out.size,
            transcendentals=0,
        ),
        name="own_part",
    )(place, *scalars, states, *prefill, *decode, w_out)


def serve_kernel(
    place_ref, partner_ref, ids_ref, count_ref, info_ref, decode_ref, slopes_ref,
    payload_ref, att_ref, dec_ref, q_ref, qd_ref, theirs_ref, normed_ref, first_ref,
):
    first_ref[...] = theirs_ref[...]
    tokens, width = q_ref.shape
    mate = partner_ref[place_ref[0]]
    prefill_slot = info_ref[0]
    length = info_ref[1]
    slots = decode_ref.shape[1]
    entries = ids_ref.shape[0]
    place = lax.broadcasted_iota(jnp.int32, (2 * slots, DK), 0)
    lands, shares = [], []
    is_prefill = jnp.zeros((2 * slots, DK), jnp.bool_)
    for row in range(slots):
        is_prefill |= (place % slots == row) & (decode_ref[0, row] == prefill_slot)
    for entry in range(entries):
        sent = entry < count_ref[mate]
        arriving = jnp.where(sent, ids_ref[entry, mate], -1)
        lands.append(arriving == prefill_slot)
        share = jnp.zeros((2 * slots, DK), jnp.float32)
        for row in range(slots):
            share = jnp.where((place % slots == row) & (decode_ref[0, row] == arriving), 1.0, share)
        shares.append(share)
    rows = lax.broadcasted_iota(jnp.int32, (tokens, DK), 0)
    later = (rows + 1).astype(jnp.float32)
    is_valid = rows < length
    for head in range(width // DK):
        here = slice(head * DK, (head + 1) * DK)
        slope = slopes_ref[head]
        chosen = jnp.zeros((DK, DK), jnp.bfloat16)
        for entry in range(entries):
            chosen = jnp.where(lands[entry], payload_ref[entry, head], chosen)
        attended = att_ref[:, here] + jnp.exp(-slope * later) * dot(q_ref[:, here], chosen)
        normed = jnp.where(is_valid, head_norm(attended), 0.0)
        normed_ref[:tokens, here] = normed.astype(jnp.bfloat16)

        keep = fade_row(-slope)
        faded = fade_row(-slope * length.astype(jnp.float32))
        queries = decode_rows(qd_ref.at[:, :, here])
        padded = jnp.concatenate([queries, queries], axis=0).astype(jnp.bfloat16)
        scale = jnp.where(place < slots, keep, keep * keep) * jnp.where(is_prefill, faded, 1.0)
        decoded = dec_ref[:, here]
        for entry in range(entries):
            seen = dot(padded, payload_ref[entry, head])[: 2 * slots]
            decoded += scale * shares[entry] * seen
        decoded = head_norm(decoded)
        padding = jnp.zeros((PAD - 2 * slots, DK), jnp.float32)
        decoded = jnp.concatenate([decoded, padding], axis=0)
        normed_ref[tokens:, here] = decoded.astype(jnp.bfloat16)


def serve(place, scalars, payload, attended, decoded, q_prefill, q_decode, theirs):
    tokens, width = q_prefill.shape
    scalar = pl.BlockSpec(memory_space=pltpu.SMEM)
    whole = pl.BlockSpec(memory_space=pltpu.VMEM)
    first = pl.BlockSpec((1, *theirs.shape[1:]), lambda i: (0, 0, 0))
    return pl.pallas_call(
        serve_kernel,
        out_shape=(
            jax.ShapeDtypeStruct((tokens + PAD, width), jnp.bfloat16),
            jax.ShapeDtypeStruct((1, *theirs.shape[1:]), theirs.dtype),
        ),
        grid=(1,),
        in_specs=[scalar] * 7 + [whole] * 5 + [first],
        out_specs=(whole, first),
        compiler_params=params(),
        name="serve",
    )(place, *scalars, payload, attended, decoded, q_prefill, q_decode, theirs)


def join_kernel(own_ref, other_ref, *refs):
    count = len(refs) // 3
    for mine_ref, theirs_ref, out_ref in zip(refs[:count], refs[count : 2 * count], refs[2 * count :]):
        total = dot(own_ref[...], mine_ref[0]) + dot(other_ref[...], theirs_ref[0])
        out_ref[...] = total.astype(jnp.bfloat16)


def join(own, other, mine, theirs, chips):
    whole = pl.BlockSpec(memory_space=pltpu.VMEM)
    count = len(chips)
    shape = (own.shape[0], mine.shape[2])
    blocks = [pl.BlockSpec((1, *mine.shape[1:]), lambda i, chip=chip: (chip, 0, 0)) for chip in chips]
    return pl.pallas_call(
        join_kernel,
        out_shape=(jax.ShapeDtypeStruct(shape, jnp.bfloat16),) * count,
        grid=(1,),
        in_specs=[whole] * 2 + blocks * 2,
        out_specs=(whole,) * count,
        compiler_params=params(),
        name=f"join{chips[0]}",
        cost_estimate=pl.CostEstimate(
            flops=4 * count * own.size * mine.shape[2],
            bytes_accessed=4 * own.size + 4 * count * mine.shape[1] * mine.shape[2],
            transcendentals=0,
        ),
    )(own, other, *[mine] * count, *[theirs] * count)


def add_kernel(a_ref, b_ref, out_ref):
    out_ref[...] = a_ref[...].astype(jnp.float32) + b_ref[...].astype(jnp.float32)


def add(a, b):
    return pl.pallas_call(
        add_kernel,
        out_shape=jax.ShapeDtypeStruct(a.shape, jnp.float32),
        compiler_params=params(0),
        name="add",
    )(a, b)


def finish_kernel(a_ref, b_ref, c_ref, prefill_ref, decode_ref):
    total = a_ref[...] + b_ref[...].astype(jnp.float32) + c_ref[...].astype(jnp.float32)
    tokens = prefill_ref.shape[0]
    prefill_ref[...] = total[:tokens].astype(jnp.bfloat16)
    steps, slots, _ = decode_ref.shape
    for step in range(steps):
        first = tokens + step * slots
        decode_ref[step] = total[first : first + slots].astype(jnp.bfloat16)


def finish(total, near, tokens, steps, slots):
    cols = total.shape[1]
    return pl.pallas_call(
        finish_kernel,
        out_shape=(
            jax.ShapeDtypeStruct((tokens, cols), jnp.bfloat16),
            jax.ShapeDtypeStruct((steps, slots, cols), jnp.bfloat16),
        ),
        compiler_params=params(0),
        name="finish",
    )(total, *near)


def siblings():
    return [(i, i ^ 1) for i in range(lax.axis_size("head"))]


def swapped(partner, array):
    return lax.cond(
        partner[0] >= 0, lambda own: lax.ppermute(own, "head", siblings()), jnp.zeros_like, array
    )


def exchange(array, pattern):
    size = lax.axis_size("replica")
    return lax.ppermute(array, "replica", [(i, i ^ pattern) for i in range(size)])


def on_device(
    states,
    partner,
    send_ids,
    send_count,
    prefill_slot,
    prompt_len,
    decode_slots,
    q_prefill,
    k_prefill,
    v_prefill,
    q_decode,
    k_decode,
    v_decode,
    slopes,
    w_out,
):
    size = lax.axis_size("replica")
    own = lax.axis_index("replica")
    head = lax.axis_index("head")
    place = jnp.stack([own, head]).astype(jnp.int32)
    ids = send_ids.T
    scalars = (partner, ids, send_count, prefill_slot, prompt_len, decode_slots, slopes)
    devices = lax.axis_size("head")

    pattern = jnp.clip(partner[0], 1, size - 1)
    half, across = size // 2, size // 4 * 3

    def hop(payload):
        return exchange(payload, across)

    payload = lax.cond(pattern >= half, hop, copied, pack(place, ids, states))

    def branch(rest, payload, *arrays):
        moving = exchange(payload, rest) if rest else copied(payload)
        attended, decoded, mine, theirs, info = own_part(*arrays)
        return moving, attended, decoded, mine, swapped(partner, theirs), info

    payload, attended, decoded, mine, theirs, info = lax.switch(
        jnp.where(pattern >= half, pattern ^ across, pattern),
        [partial(branch, rest) for rest in range(half)],
        payload,
        place,
        scalars,
        states,
        (q_prefill, k_prefill, v_prefill),
        (q_decode, k_decode, v_decode),
        w_out,
    )
    scalars = (partner, ids, send_count, info, decode_slots, slopes)
    normed, first = serve(
        place, scalars, payload, attended, decoded, q_prefill, q_decode, theirs
    )
    other = lax.ppermute(normed, "head", siblings())

    def along(part, away):
        return lax.ppermute(part, "head", [(i, (i + 2 * away) % devices) for i in range(devices)])

    (farthest,) = join(normed, other, mine, first, (0,))
    farthest, normed = lax.optimization_barrier((farthest, normed))
    *near, here = join(normed, other, mine, theirs, (1, 2, 3))
    near = [along(part, away) for part, away in zip(near, ORDER[1:-1], strict=True)]
    total = add(along(farthest, ORDER[0]), here)
    steps, slots = q_decode.shape[:2]
    return finish(total, near, q_prefill.shape[0], steps, slots)


def solution(mesh):
    return jax.shard_map(
        on_device,
        mesh=mesh,
        in_specs=(
            P("replica", "head", None, None),
            P(),
            P(),
            P(),
            P("replica"),
            P("replica"),
            P("replica", None),
            P("replica", "head"),
            P("replica", "head"),
            P("replica", "head"),
            P(None, "replica", "head"),
            P(None, "replica", "head"),
            P(None, "replica", "head"),
            P("head"),
            P("head", None),
        ),
        out_specs=(P("replica", "head"), P(None, "replica", "head")),
        check_vma=False,
    )
```
